256 devices in a mesh: ctx: 64 (over z_lo, x, y), tp: 4 (over z_hi, core).
Axes of the slice: x: 4, y: 4, z: 8 (z_hi: 2, z_lo: 4; z = z_hi * 4 + z_lo), core: 2. Of those that a mesh axis runs over, the one named last changes fastest.
Arguments:
- step_inputs: bfloat16 [8192, 8192], P('ctx', 'tp'), may hold values from -6 to 6
- log_decay: float32 [8192, 128], P('ctx', 'tp'), may hold values from -0.7 to 0
- write_vecs: bfloat16 [8192, 2048], P('ctx', 'tp'), may hold values from -6 to 6
- read_vecs: bfloat16 [8192, 2048], P('ctx', 'tp'), may hold values from -0.375 to 0.375
- gate_vals: bfloat16 [8192, 8192], P('ctx', 'tp'), may hold values from -6 to 6
- skip_gain: float32 [128], P('tp'), may hold values from 0.5 to 2
- norm_gain: float32 [8192], P('tp'), may hold values from 0.5 to 1.5
- query_rows: bfloat16 [8192, 4096], P('ctx', 'tp'), may hold values from -160 to 160
- key_rows: bfloat16 [8192, 1024], P('ctx', 'tp'), may hold values from -6 to 6
- value_rows: bfloat16 [8192, 1024], P('ctx', 'tp'), may hold values from -6 to 6
Outputs:
- mamba_out: bfloat16 [8192, 8192], P('ctx', 'tp')
- attn_out: bfloat16 [8192, 4096], P('ctx', 'tp')
The draws below stay inside these ranges and needn't reach their ends.
All inputs are finite; a program needn't handle non-finite values.
Results may differ from the reference program's by a relative error of at most 0.0049.
Values may be sent and summed in bfloat16 or wider, within the bound.
No kernel may reach another device: no remote copies, remote signals or barrier semaphores. Data moves between devices by JAX's collectives and lax.ppermute only.
A program may use at most 320 MiB of HBM per device.

```python
import math
import jax
import jax.numpy as jnp
from jax import lax

L_DEV = 128
MHEADS = 128
MHDIM = 64
NSTATE = 256
NGROUPS = 8
QHEADS = 32
KVHEADS = 8
HDIM = 128
SEQUENCE_LENGTH = 8192


def head_rates(key, slow_odds):
    flag_key, fast_key, slow_key = jax.random.split(key, 3)
    slow_flag = jax.random.randint(flag_key, (MHEADS,), 0, slow_odds) != 0
    fast_rate = jnp.exp(jax.random.uniform(fast_key, (MHEADS,), jnp.float32, math.log(1.0 / 50.0), math.log(1.0 / 30.0)))
    slow_rate = jnp.exp(jax.random.uniform(slow_key, (MHEADS,), jnp.float32, math.log(0.3), math.log(0.6))) / SEQUENCE_LENGTH
    return jnp.where(slow_flag, slow_rate, fast_rate)


def draw_log_decay(key, part):
    head_rate = head_rates(key, 2)
    key = jax.random.fold_in(key, 11)
    coarse_random_key, device_random_key, spike_random_key, depth_random_key = jax.random.split(key, 4)
    rough = jnp.exp(jax.random.uniform(coarse_random_key, (SEQUENCE_LENGTH, MHEADS), jnp.float32, math.log(0.5), math.log(2.0)))
    device_factor = jnp.exp(jax.random.uniform(device_random_key, (SEQUENCE_LENGTH // L_DEV, 1, MHEADS), jnp.float32, math.log(0.5), math.log(2.0)))
    device_factor = jnp.broadcast_to(device_factor, (SEQUENCE_LENGTH // L_DEV, L_DEV, MHEADS)).reshape(SEQUENCE_LENGTH, MHEADS)
    step_logarithm = -(head_rate[None, :] * rough * device_factor)
    spike_position = jax.random.randint(spike_random_key, (2,), 0, SEQUENCE_LENGTH)
    spike_depth = -jax.random.uniform(depth_random_key, (2,), jnp.float32, 0.22, 0.69)
    spike_flag = jnp.arange(SEQUENCE_LENGTH)[:, None] == spike_position[None, :]
    spike_values = jnp.min(jnp.where(spike_flag, spike_depth[None, :], 0.0), axis=1)
    return jnp.minimum(step_logarithm, spike_values[:, None]).astype(jnp.float32)


def draw_step_inputs(key, part):
    head_rate = head_rates(key, 2)
    key = jax.random.fold_in(key, 12)
    head_scale = jnp.sqrt(head_rate * 40.0)
    raw_vals = jnp.clip(jax.random.normal(key, (SEQUENCE_LENGTH, MHEADS, MHDIM), jnp.float32), -5.0, 5.0)
    return (raw_vals * head_scale[None, :, None]).reshape(SEQUENCE_LENGTH, MHEADS * MHDIM).astype(jnp.bfloat16)


def aligned_keys(key):
    normal_key = jax.random.fold_in(key, 0)
    key_table = jnp.clip(jax.random.normal(normal_key, (SEQUENCE_LENGTH, KVHEADS * HDIM), jnp.float32), -6.0, 6.0)
    for slot_index in range(4):
        source = (slot_index + 1) * SEQUENCE_LENGTH // 8
        target = source + SEQUENCE_LENGTH // 16
        key_table = key_table.at[target].set(key_table[target])
    return key_table


def draw_key_rows(key, part):
    key_table = aligned_keys(key)
    return key_table.astype(jnp.bfloat16)


def draw_query_rows(key, part):
    key = jax.random.fold_in(key, 21)
    query_table = jnp.clip(jax.random.normal(key, (SEQUENCE_LENGTH, QHEADS * HDIM), jnp.float32), -6.0, 6.0)
    return query_table.astype(jnp.bfloat16)


def block_scale(own_key, extent, cuts, low, high):
    gain = 1.0
    for dim, parts in cuts:
        steps = jax.random.uniform(jax.random.fold_in(jax.random.fold_in(own_key, 6), dim), (parts,), jnp.float32, low / len(cuts), high / len(cuts))
        gain = gain * jnp.repeat(jnp.exp(steps), extent[dim] // parts).reshape((-1,) + (1,) * (len(extent) - 1 - dim))
    return gain


def normal_values(key, dims, spread, limit, shards=(), held_as=jnp.bfloat16):
    result = spread * jax.random.normal(key, dims, jnp.float32)
    if shards:
        result = result * block_scale(key, dims, shards, -0.22, 0.18)
    return jnp.clip(result, -limit, limit).astype(held_as)


def setup_inputs(seed: int = 0) -> dict:
    arg_keys = jax.random.split(jax.random.key(seed), 11)
    step_inputs = draw_step_inputs(jax.random.fold_in(arg_keys[10], 71), 0)
    log_decay = draw_log_decay(jax.random.fold_in(arg_keys[10], 71), 0)
    write_vecs = normal_values(arg_keys[2], (SEQUENCE_LENGTH, NGROUPS * NSTATE), 1.0, 6.0, ((0, 64), (1, 4)))
    read_vecs = normal_values(arg_keys[3], (SEQUENCE_LENGTH, NGROUPS * NSTATE), NSTATE ** -0.5, 0.375, ((0, 64), (1, 4)))
    gate_vals = normal_values(arg_keys[4], (SEQUENCE_LENGTH, MHEADS * MHDIM), 1.0, 6.0, ((0, 64), (1, 4)))
    skip_gain = jnp.clip(0.5 + 1.5 * jax.random.uniform(arg_keys[5], (MHEADS,), jnp.float32) ** block_scale(arg_keys[5], (MHEADS,), ((0, 4),), -0.2, 0.2), 0.5, 2.0)
    norm_gain = jnp.clip(1.0 + 0.1 * jax.random.normal(arg_keys[6], (MHEADS * MHDIM,), jnp.float32), 0.5, 1.5)
    query_rows = draw_query_rows(jax.random.fold_in(arg_keys[10], 71), 0)
    key_rows = draw_key_rows(jax.random.fold_in(arg_keys[10], 71), 0)
    value_rows = normal_values(arg_keys[9], (SEQUENCE_LENGTH, KVHEADS * HDIM), 1.0, 6.0, ((0, 64), (1, 4)))
    return {"step_inputs": step_inputs, "log_decay": log_decay, "write_vecs": write_vecs, "read_vecs": read_vecs, "gate_vals": gate_vals, "skip_gain": skip_gain, "norm_gain": norm_gain, "query_rows": query_rows, "key_rows": key_rows, "value_rows": value_rows}


eps_norm = 1e-05
neg_large = -1e+30

def ssd_block(carried, block):
    inputs_grid, decay_log, write_grid, read_grid = block
    length = decay_log.shape[0]
    groups = write_grid.shape[1]
    per_group = decay_log.shape[1] // groups
    cumulative = jnp.cumsum(decay_log, axis=0)
    last_cum = cumulative[length - 1]
    positions = jnp.arange(length, dtype=jnp.int32)
    causal_mask = positions[:, None] >= positions[None, :]
    pair_dots = jnp.einsum('tgn,sgn->gts', read_grid.astype(jnp.float32), write_grid.astype(jnp.float32))
    cum_gaps = cumulative.T[:, :, None] - cumulative.T[:, None, :]
    decays = jnp.where(causal_mask[None], jnp.exp(jnp.where(causal_mask[None], cum_gaps, 0.0)), 0.0)
    weights = (decays.reshape(groups, per_group, length, length) * pair_dots[:, None]).astype(jnp.bfloat16)
    local_out = jnp.einsum('ghts,sghp->tghp', weights.astype(jnp.float32), inputs_grid.astype(jnp.float32))
    tail_decay = jnp.exp(last_cum[None, :] - cumulative).reshape(length, groups, per_group, 1)
    decayed = (inputs_grid * tail_decay).astype(jnp.bfloat16)
    block_state = jnp.einsum('sghp,sgn->ghpn', decayed.astype(jnp.float32), write_grid.astype(jnp.float32))
    carried_grid = carried.reshape(groups, per_group, MHDIM, NSTATE)
    inflow = jnp.einsum('tgn,ghpn->tghp', read_grid.astype(jnp.float32), carried_grid, precision=lax.Precision.HIGHEST)
    inflow = inflow * jnp.exp(cumulative).reshape(length, groups, per_group, 1)
    new_state = jnp.exp(last_cum)[:, None, None] * carried + block_state.reshape(carried.shape)
    return (new_state, (local_out, inflow))

def attend_head(head_index, query_rows, key_rows, value_rows):
    group_share = QHEADS // KVHEADS
    query_head = lax.dynamic_slice_in_dim(query_rows, (head_index * HDIM).astype(jnp.int32), HDIM, 1)
    kv_start = (head_index // group_share * HDIM).astype(jnp.int32)
    key_head = lax.dynamic_slice_in_dim(key_rows, kv_start, HDIM, 1)
    value_head = lax.dynamic_slice_in_dim(value_rows, kv_start, HDIM, 1)
    block_rows = min(512, SEQUENCE_LENGTH)
    key_pos = jnp.arange(SEQUENCE_LENGTH, dtype=jnp.int32)

    def one_block(start):
        query_block = lax.dynamic_slice_in_dim(query_head, start.astype(jnp.int32), block_rows, 0)
        scores = jnp.dot(query_block, key_head.T, preferred_element_type=jnp.float32) * HDIM ** (-0.5)
        query_pos = start.astype(jnp.int32) + jnp.arange(block_rows, dtype=jnp.int32)
        allowed = key_pos[None, :] <= query_pos[:, None]
        scores = jnp.where(allowed, scores, neg_large)
        top_score = lax.optimization_barrier(jnp.max(scores, axis=1, keepdims=True))
        expo_weights = jnp.where(allowed, jnp.exp(scores - top_score), 0.0)
        totals = lax.optimization_barrier(jnp.sum(expo_weights, axis=1))
        summed = jnp.dot(expo_weights.astype(jnp.bfloat16), value_head, preferred_element_type=jnp.float32)
        return (summed / totals[:, None]).astype(jnp.bfloat16)
    starts = jnp.arange(SEQUENCE_LENGTH // block_rows, dtype=jnp.int32) * block_rows
    return lax.map(one_block, starts).reshape(SEQUENCE_LENGTH, HDIM)

def reference(step_inputs, log_decay, write_vecs, read_vecs, gate_vals, skip_gain, norm_gain, query_rows, key_rows, value_rows):
    blocks = SEQUENCE_LENGTH // L_DEV
    per_group = MHEADS // NGROUPS
    inputs_grid = step_inputs.reshape(blocks, L_DEV, NGROUPS, per_group, MHDIM)
    decay_grid = log_decay.reshape(blocks, L_DEV, MHEADS)
    write_grid = write_vecs.reshape(blocks, L_DEV, NGROUPS, NSTATE)
    read_grid = read_vecs.reshape(blocks, L_DEV, NGROUPS, NSTATE)
    start_state = jnp.zeros((MHEADS, MHDIM, NSTATE), jnp.float32)
    _, parts_out = lax.scan(ssd_block, start_state, (inputs_grid, decay_grid, write_grid, read_grid))
    local_out, inflow = parts_out
    mixed_out = local_out + inflow + skip_gain.reshape(NGROUPS, per_group, 1) * inputs_grid
    gated_vals = mixed_out.reshape(SEQUENCE_LENGTH, MHEADS * MHDIM) * jax.nn.silu(gate_vals.astype(jnp.float32))
    group_vals = gated_vals.reshape(SEQUENCE_LENGTH, NGROUPS, per_group * MHDIM)
    squares = lax.optimization_barrier(jnp.mean(group_vals * group_vals, axis=2, keepdims=True))
    normed = (group_vals * lax.rsqrt(squares + eps_norm)).reshape(SEQUENCE_LENGTH, MHEADS * MHDIM)
    mamba_out = (normed * norm_gain).astype(jnp.bfloat16)

    def per_head(head_index):
        return attend_head(head_index, query_rows, key_rows, value_rows)
    heads_out = lax.map(per_head, jnp.arange(QHEADS, dtype=jnp.int32))
    attn_out = jnp.transpose(heads_out, (1, 0, 2)).reshape(SEQUENCE_LENGTH, QHEADS * HDIM)
    return (mamba_out, attn_out)
```

```python
import functools

import jax
import jax.numpy as jnp
from jax import lax
from jax.experimental import pallas as pl
from jax.experimental.pallas import tpu as pltpu
from jax.sharding import PartitionSpec as P

MHDIM = 64
NSTATE = 256
HDIM = 128
LBLK = 128
SLICE = 512
KVW = 2 * HDIM
TILE = 256

eps_norm = 1e-05
neg_large = -1e30
score_scale = HDIM ** (-0.5) * 1.4426950408889634

bf16 = jnp.bfloat16
f32 = jnp.float32
HIGHEST = lax.Precision.HIGHEST


def shape(dims, dtype):
    return jax.ShapeDtypeStruct(dims, dtype)


def run(kernel, outs, args, scratch=(), flops=1000000, moved=1000000):
    vmem = pl.BlockSpec(memory_space=pltpu.VMEM)
    smem = pl.BlockSpec(memory_space=pltpu.SMEM)
    return pl.pallas_call(
        kernel,
        out_shape=outs,
        in_specs=[smem] + [vmem] * (len(args) - 1),
        out_specs=[vmem] * len(outs),
        scratch_shapes=list(scratch),
        compiler_params=pltpu.CompilerParams(vmem_limit_bytes=40 * 1024 * 1024),
        cost_estimate=pl.CostEstimate(flops=flops, bytes_accessed=moved, transcendentals=0),
    )(*args)


def ring4(place, shift):
    return lax.bitwise_and(place + shift, 3)


def lanes(start, size):
    return pl.ds(pl.multiple_of(start * size, size), size)


def split3(vals):
    high = vals.astype(bf16)
    rest = vals - high.astype(f32)
    mid = rest.astype(bf16)
    low = (rest - mid.astype(f32)).astype(bf16)
    return high, mid, low


def iota(dims, dim):
    return lax.broadcasted_iota(jnp.int32, dims, dim)


def pack_kernel(place, x, b, c, decay, q, k, v, *outs):
    y = place[2]
    xbc, (q_same, q_other, kv_own, kv_other) = outs[:4], outs[4:]
    lane = iota((LBLK, 128), 1)
    for s in range(4):
        j = ring4(y, s)
        group = lax.shift_right_logical(j, 1)
        xbc[s][:, 0:SLICE] = x[:, lanes(j, SLICE)]
        xbc[s][:, SLICE : SLICE + NSTATE] = b[:, lanes(group, NSTATE)]
        xbc[s][:, SLICE + NSTATE : SLICE + 2 * NSTATE] = c[:, lanes(group, NSTATE)]
        high, mid, low = split3(decay[:, lanes(j, 128)])
        part = jnp.where(lane < 8, high.astype(f32), jnp.where(lane < 16, mid.astype(f32), low.astype(f32)))
        xbc[s][:, SLICE + 2 * NSTATE :] = part.astype(bf16)
    head = lax.bitwise_and(y, 1)
    other = 1 - head
    q_same[...] = q[:, lanes(head, 4 * HDIM)]
    q_other[...] = q[:, lanes(other, 4 * HDIM)]
    kv_own[:, :HDIM] = k[:, lanes(head, HDIM)]
    kv_own[:, HDIM:] = v[:, lanes(head, HDIM)]
    kv_other[:, :HDIM] = k[:, lanes(other, HDIM)]
    kv_other[:, HDIM:] = v[:, lanes(other, HDIM)]


def block_decays(decay_parts):
    tri = (iota((LBLK, LBLK), 0) >= iota((LBLK, LBLK), 1)).astype(f32).astype(bf16)
    cum_parts = jnp.dot(tri, decay_parts, preferred_element_type=f32)
    row = iota((128, SLICE), 0)
    spread = jnp.where(
        (lax.bitwise_and(row, 7) == lax.shift_right_logical(iota((128, SLICE), 1), 6)) & (row < 24), 1.0, 0.0
    )
    return tri, cum_parts, jnp.dot(cum_parts, spread, precision=HIGHEST, preferred_element_type=f32)


def block_sum(block, cum):
    last = cum[LBLK - 1 : LBLK, :]
    decayed = (block[:, 0:SLICE].astype(f32) * jnp.exp(last - cum)).astype(bf16)
    state = lax.dot_general(
        block[:, SLICE : SLICE + NSTATE], decayed, (((0,), (0,)), ((), ())), preferred_element_type=f32
    )
    return state, last


def write_total(out, state, log_total):
    out[0:NSTATE, :] = state.astype(bf16)
    high, mid, low = split3(log_total)
    row = iota((16, log_total.shape[1]), 0)
    out[NSTATE:, :] = jnp.where(
        row == 0,
        high.astype(f32),
        jnp.where(row == 1, mid.astype(f32), jnp.where(row == 2, low.astype(f32), 0.0)),
    ).astype(bf16)


def read_total(vals):
    tail = vals[NSTATE:, :].astype(f32)
    return vals[0:NSTATE, :].astype(f32), tail[0:1] + tail[1:2] + tail[2:3]


def total_kernel(place, r0, r1, r2, r3, t0, t1, t2, t3, ordered, total):
    x, y = place[1], place[2]
    for s, r in enumerate((r0, r1, r2, r3)):
        ordered[ring4(y, -s)] = r[...]
    log_total = jnp.zeros((1, SLICE), f32)
    for block in range(4):
        _, _, cum = block_decays(ordered[block, :, SLICE + 2 * NSTATE :])
        state, last = block_sum(ordered[block], cum)
        log_total = log_total + last
        total[...] = state if block == 0 else jnp.exp(last) * total[...] + state
    logs = jnp.broadcast_to(log_total, (8, SLICE))
    ordered_log = logs
    total_log = ordered_log[0:1]
    for s, t in enumerate((t0, t1, t2, t3)):
        j = ring4(x, s)
        log_part = jnp.where(
            j == 0,
            total_log[:, 0:128],
            jnp.where(j == 1, total_log[:, 128:256], jnp.where(j == 2, total_log[:, 256:384], total_log[:, 384:512])),
        )
        write_total(t, total[:, lanes(j, 128)], log_part)


def plane_kernel(place, r0, r1, r2, r3, out, ordered):
    x = place[1]
    for s, r in enumerate((r0, r1, r2, r3)):
        ordered[ring4(x, -s)] = r[...]
    total, log_total = read_total(ordered[0])
    for block in range(1, 4):
        state, last = read_total(ordered[block])
        total = jnp.exp(last) * total + state
        log_total = log_total + last
    write_total(out, total, log_total)


def entering_kernel(place, r0, r1, r2, r3, up1, up2, up3, g0, g1, g2, g3, ordered, entering):
    x = place[1]
    for s, r in enumerate((r0, r1, r2, r3)):
        ordered[ring4(x, -s)] = r[...]
    current, _ = read_total(up3[...])
    for up in (up2, up1):
        state, last = read_total(up[...])
        current = jnp.exp(last) * current + state
    for block in range(4):
        entering[block] = current.astype(bf16)
        if block < 3:
            state, last = read_total(ordered[block])
            current = jnp.exp(last) * current + state
    for s, g in enumerate((g0, g1, g2, g3)):
        g[...] = entering[ring4(x, s)]


def mixed_kernel(place, r0, r1, r2, r3, g0, g1, g2, g3, skip, m0, m1, m2, m3, ordered, carried, results):
    x, y = place[1], place[2]
    for s, r in enumerate((r0, r1, r2, r3)):
        ordered[ring4(y, -s)] = r[...]
    for s, g in enumerate((g0, g1, g2, g3)):
        carried[:, lanes(ring4(x, -s), 128)] = g[...].astype(f32)
    gain = skip[:, lanes(y, SLICE)]
    causal = iota((LBLK, LBLK), 0) >= iota((LBLK, LBLK), 1)
    low_half = iota((LBLK, 128), 1) < MHDIM
    for block in range(4):
        vals = ordered[block]
        decay_parts = vals[:, SLICE + 2 * NSTATE :]
        tri, cum_parts, cum = block_decays(decay_parts)
        row_parts = lax.dot_general(decay_parts, tri, (((0,), (1,)), ((), ())), preferred_element_type=f32)
        cum_rows = row_parts[0:8] + row_parts[8:16] + row_parts[16:24]
        cum_cols = cum_parts[:, 0:8] + cum_parts[:, 8:16] + cum_parts[:, 16:24]
        write, read = vals[:, SLICE : SLICE + NSTATE], vals[:, SLICE + NSTATE : SLICE + 2 * NSTATE]
        pair_dots = lax.dot_general(read, write, (((1,), (1,)), ((), ())), preferred_element_type=f32)
        held = carried[...]
        held_high = held.astype(bf16)
        held_low = (held - held_high.astype(f32)).astype(bf16)
        inflow = jnp.dot(read, held_high, preferred_element_type=f32) + jnp.dot(
            read, held_low, preferred_element_type=f32
        )
        for pair in range(4):
            part = slice(pair * 128, pair * 128 + 128)
            xs = vals[:, part]
            locals_ = []
            for head in (2 * pair, 2 * pair + 1):
                gap = cum_cols[:, head : head + 1] - cum_rows[head : head + 1, :]
                decays = jnp.exp(jnp.where(causal, gap, neg_large))
                weight = (decays * pair_dots).astype(bf16)
                locals_.append(jnp.dot(weight, xs, preferred_element_type=f32))
            local = jnp.where(low_half, locals_[0], locals_[1])
            mixed = local + jnp.exp(cum[:, part]) * inflow[:, part] + gain[:, part] * xs.astype(f32)
            results[block, :, part] = mixed.astype(bf16)
        if block < 3:
            state, last = block_sum(vals, cum)
            carried[...] = jnp.exp(last) * held + state
    for s, m in enumerate((m0, m1, m2, m3)):
        m[...] = results[ring4(y, s)]


def norm_kernel(place, m0, m1, m2, m3, gate, gain, out):
    y = place[2]
    gated, squares, groups, slots = [], [], [], []
    for s, m in enumerate((m0, m1, m2, m3)):
        j = ring4(y, -s)
        gates = gate[:, lanes(j, SLICE)].astype(f32)
        vals = m[...].astype(f32) * (gates / (1.0 + jnp.exp(-gates)))
        gated.append(vals)
        squares.append(jnp.sum(vals * vals, axis=1, keepdims=True))
        groups.append(lax.shift_right_logical(j, 1))
        slots.append(j)
    for s in range(4):
        total = jnp.zeros((LBLK, 1), f32)
        for other in range(4):
            total = total + jnp.where(groups[other] == groups[s], squares[other], 0.0)
        factor = lax.rsqrt(total * (1.0 / 1024.0) + eps_norm)
        out[:, lanes(slots[s], SLICE)] = (gated[s] * factor * gain[:, lanes(slots[s], SLICE)]).astype(bf16)


def attend(tile, q, keys, values, tops, sums, acc, masks=None):
    rows = pl.ds(pl.multiple_of(tile * TILE, TILE), TILE)
    queries = q[rows, :]
    scores = [
        lax.dot_general(queries, key, (((1,), (1,)), ((), ())), preferred_element_type=f32) for key in keys
    ]
    if masks is not None:
        scores = [jnp.where(mask, score, neg_large) for mask, score in zip(masks, scores)]
    top = functools.reduce(jnp.maximum, scores)
    held_top = tops[rows, 0:1]
    new_top = jnp.maximum(held_top, jnp.max(top, axis=1, keepdims=True))
    expos = [jnp.exp2((score - new_top) * score_scale) for score in scores]
    if masks is not None:
        expos = [jnp.where(mask, expo, 0.0) for mask, expo in zip(masks, expos)]
    factor = jnp.exp2((held_top - new_top) * score_scale)
    total = jnp.sum(functools.reduce(jnp.add, expos), axis=1, keepdims=True)
    summed = functools.reduce(
        jnp.add,
        [jnp.dot(expo.astype(bf16), value, preferred_element_type=f32) for expo, value in zip(expos, values)],
    )
    tops[rows, :] = jnp.broadcast_to(new_top, (TILE, 128))
    sums[rows, :] = jnp.broadcast_to(sums[rows, 0:1] * factor + total, (TILE, 128))
    acc[rows, :] = acc[rows, :] * factor + summed


def own_kernel(place, q0, q1, q2, q3, kv_own, kv_recv, q, tops, sums, acc):
    y = place[2]
    for s, part in enumerate((q0, q1, q2, q3)):
        for head in range(4):
            start = (s * 4 + head) * LBLK
            q[start : start + LBLK, :] = part[:, head * HDIM : (head + 1) * HDIM]
    tops[...] = jnp.full(tops.shape, neg_large, f32)
    sums[...] = jnp.zeros(sums.shape, f32)
    acc[...] = jnp.zeros(acc.shape, f32)
    keys = [kv_own[:, :HDIM], kv_recv[:, :HDIM]]
    values = [kv_own[:, HDIM:], kv_recv[:, HDIM:]]

    def step(tile, _):
        block = ring4(y, -lax.shift_right_logical(tile, 1))
        query_pos = block * LBLK + lax.bitwise_and(iota((TILE, LBLK), 0), LBLK - 1)
        key_pos = iota((TILE, LBLK), 1)
        masks = [key_pos + y * LBLK <= query_pos, key_pos + lax.bitwise_xor(y, 1) * LBLK <= query_pos]
        attend(tile, q, keys, values, tops, sums, acc, masks)
        return 0

    lax.fori_loop(0, q.shape[0] // TILE, step, 0)


def copy_state(old, new):
    for old_ref, new_ref in zip(old, new):
        new_ref[...] = old_ref[...]


def row_kernel(place, q, tops, sums, acc, kv1, kv2, kv3, new_tops, new_sums, new_acc):
    x = place[1]
    copy_state((tops, sums, acc), (new_tops, new_sums, new_acc))
    for s, kv in enumerate((kv1, kv2, kv3)):

        @pl.when(ring4(x, -(s + 1)) < x)
        def _(kv=kv):
            def step(tile, _):
                attend(tile, q, [kv[:, :HDIM]], [kv[:, HDIM:]], new_tops, new_sums, new_acc)
                return 0

            lax.fori_loop(0, q.shape[0] // TILE, step, 0)


def plane_attend(distance, place, q, tops, sums, acc, kv0, kv1, kv2, kv3, new_tops, new_sums, new_acc):
    copy_state((tops, sums, acc), (new_tops, new_sums, new_acc))

    @pl.when(place[0] >= distance)
    def _():
        blocks = (kv0, kv1, kv2, kv3)

        def step(tile, _):
            attend(
                tile,
                q,
                [kv[:, :HDIM] for kv in blocks],
                [kv[:, HDIM:] for kv in blocks],
                new_tops,
                new_sums,
                new_acc,
            )
            return 0

        lax.fori_loop(0, q.shape[0] // TILE, step, 0)


def finish_kernel(place, tops, sums, acc, o0, o1, o2, o3):
    lane = iota((LBLK, 128), 1)
    for s, o in enumerate((o0, o1, o2, o3)):
        stats = jnp.zeros((LBLK, 128), f32)
        for head in range(4):
            start = (s * 4 + head) * LBLK
            rows = slice(start, start + LBLK)
            total = sums[rows, :]
            o[:, head * HDIM : (head + 1) * HDIM] = (acc[rows, :] / jnp.where(total > 0, total, 1.0)).astype(bf16)
            for place_in, part in enumerate(split3(tops[rows, :]) + split3(total)):
                stats = jnp.where(lane == head * 6 + place_in, part.astype(f32), stats)
        o[:, 4 * HDIM :] = stats.astype(bf16)


def merge_kernel(place, o0, o1, o2, o3, out):
    head_group = lax.bitwise_and(place[2], 1)
    for pair, group in (((o0, o2), head_group), ((o1, o3), 1 - head_group)):
        merged = []
        stats = [part[:, 4 * HDIM :].astype(f32) for part in pair]
        for head in range(4):
            tops, sums = [], []
            for stat in stats:
                cols = [stat[:, head * 6 + i : head * 6 + i + 1] for i in range(6)]
                tops.append(cols[0] + cols[1] + cols[2])
                sums.append(cols[3] + cols[4] + cols[5])
            top = jnp.maximum(tops[0], tops[1])
            weights = [total * jnp.exp2((one - top) * score_scale) for one, total in zip(tops, sums)]
            whole = weights[0] + weights[1]
            vals = [part[:, head * HDIM : (head + 1) * HDIM].astype(f32) for part in pair]
            merged.append((vals[0] * (weights[0] / whole) + vals[1] * (weights[1] / whole)).astype(bf16))
        out[:, lanes(group, 4 * HDIM)] = jnp.concatenate(merged, axis=1)


def shift_y(vals, shift):
    return lax.ppermute(vals, "ctx", [(i, (i & ~3) | ((i + shift) & 3)) for i in range(64)])


def shift_x(vals, shift):
    return lax.ppermute(vals, "ctx", [(i, (i & ~12) | ((i + 4 * shift) & 12)) for i in range(64)])


def up_z(vals, shift):
    return lax.ppermute(vals, "ctx", [(i, i + 16 * shift) for i in range(64 - 16 * shift)])


def on_device(
    step_inputs, log_decay, write_vecs, read_vecs, gate_vals, skip_gain, norm_gain, query_rows, key_rows, value_rows
):
    index = lax.axis_index("ctx").astype(jnp.int32)
    place = jnp.stack([index // 16, (index // 4) % 4, index % 4, index])
    decay_copies = jnp.tile(log_decay.reshape(LBLK, 4, 1, 8), (1, 1, 3, 1)).reshape(LBLK, 4, 24)
    decay_grid = jnp.pad(decay_copies, ((0, 0), (0, 0), (0, 104))).reshape(LBLK, 512)
    skip = jnp.repeat(skip_gain, MHDIM).reshape(1, 4 * SLICE)
    gain = norm_gain.reshape(1, 4 * SLICE)

    width = SLICE + 2 * NSTATE + 128
    packed = run(
        pack_kernel,
        [shape((LBLK, width), bf16)] * 4 + [shape((LBLK, 4 * HDIM), bf16)] * 2 + [shape((LBLK, KVW), bf16)] * 2,
        (place, step_inputs, write_vecs, read_vecs, decay_grid, query_rows, key_rows, value_rows),
        moved=3 << 20,
    )
    xbc, (q_same, q_other, kv_own, kv_other) = packed[:4], packed[4:]
    kv_recv = lax.ppermute(kv_other, "ctx", [(i, i ^ 1) for i in range(64)])
    blocks = [xbc[0]] + [shift_y(xbc[s], s) for s in (1, 2, 3)]
    queries = [q_same, shift_y(q_other, 1), shift_y(q_same, 2), shift_y(q_other, 3)]

    kv = jnp.concatenate([kv_own, kv_recv], axis=0)
    planes = [kv] + [up_z(kv, s) for s in (1, 2, 3)]
    columns = [[one] + [shift_x(one, s) for s in (1, 2, 3)] for one in planes]

    totals = run(
        total_kernel,
        [shape((NSTATE + 16, 128), bf16)] * 4,
        (place, *blocks),
        [pltpu.VMEM((4, LBLK, width), bf16), pltpu.VMEM((NSTATE, SLICE), f32)],
        flops=600 << 20,
        moved=2 << 20,
    )
    totals = [totals[0]] + [shift_x(totals[s], s) for s in (1, 2, 3)]
    (plane_total,) = run(
        plane_kernel,
        [shape((NSTATE + 16, 128), bf16)],
        (place, *totals),
        [pltpu.VMEM((4, NSTATE + 16, 128), bf16)],
        moved=1 << 20,
    )
    ups = [up_z(plane_total, s) for s in (1, 2, 3)]
    entering = run(
        entering_kernel,
        [shape((NSTATE, 128), bf16)] * 4,
        (place, *totals, *ups),
        [pltpu.VMEM((4, NSTATE + 16, 128), bf16), pltpu.VMEM((4, NSTATE, 128), bf16)],
        moved=1 << 20,
    )
    entering = [entering[0]] + [shift_x(entering[s], s) for s in (1, 2, 3)]
    mixed = run(
        mixed_kernel,
        [shape((LBLK, SLICE), bf16)] * 4,
        (place, *blocks, *entering, skip),
        [
            pltpu.VMEM((4, LBLK, width), bf16),
            pltpu.VMEM((NSTATE, SLICE), f32),
            pltpu.VMEM((4, LBLK, SLICE), bf16),
        ],
        flops=2 << 30,
        moved=4 << 20,
    )
    mixed = [mixed[0]] + [shift_y(mixed[s], s) for s in (1, 2, 3)]
    (mamba_out,) = run(
        norm_kernel, [shape((LBLK, 4 * SLICE), bf16)], (place, *mixed, gate_vals, gain), moved=4 << 20
    )

    rows = 16 * LBLK
    state_shapes = [shape((rows, 128), f32)] * 3
    unit = 4 * rows * KVW * HDIM
    q, *state = run(
        own_kernel,
        [shape((rows, HDIM), bf16)] + state_shapes,
        (place, *queries, kv_own, kv_recv),
        flops=8 * unit,
        moved=8 << 20,
    )
    state = run(row_kernel, state_shapes, (place, q, *state, *columns[0][1:]), flops=24 * unit, moved=8 << 20)
    for distance in (1, 2, 3):
        state = run(
            functools.partial(plane_attend, distance),
            state_shapes,
            (place, q, *state, *columns[distance]),
            flops=32 * unit,
            moved=8 << 20,
        )
    outs = run(finish_kernel, [shape((LBLK, 4 * HDIM + 128), bf16)] * 4, (place, *state), moved=4 << 20)
    outs = [outs[0]] + [shift_y(outs[s], -s) for s in (1, 2, 3)]
    (attn_out,) = run(merge_kernel, [shape((LBLK, 8 * HDIM), bf16)], (place, *outs), moved=2 << 20)
    return (mamba_out, attn_out)


def solution(mesh):
    in_specs = (
        P("ctx", "tp"),
        P("ctx", "tp"),
        P("ctx", "tp"),
        P("ctx", "tp"),
        P("ctx", "tp"),
        P("tp"),
        P("tp"),
        P("ctx", "tp"),
        P("ctx", "tp"),
        P("ctx", "tp"),
    )
    out_specs = (P("ctx", "tp"), P("ctx", "tp"))
    return jax.shard_map(on_device, mesh=mesh, in_specs=in_specs, out_specs=out_specs, check_vma=False)
```

```python
import functools

import jax
import jax.numpy as jnp
from jax import lax
from jax.experimental import pallas as pl
from jax.experimental.pallas import tpu as pltpu
from jax.sharding import PartitionSpec as P

MHDIM = 64
NSTATE = 256
HDIM = 128
LBLK = 128
SLICE = 512
KVW = 2 * HDIM
AT_B = SLICE
AT_C = AT_B + NSTATE
AT_DECAY = AT_C + NSTATE
AT_Q = AT_DECAY + 128
WIDTH = AT_Q + 4 * HDIM

eps_norm = 1e-05
neg_large = -1e30
no_top = -1e29
score_scale = HDIM ** (-0.5) * 1.4426950408889634

bf16 = jnp.bfloat16
f32 = jnp.float32


def shape(dims, dtype):
    return jax.ShapeDtypeStruct(dims, dtype)


def run(kernel, outs, args, scratch=(), flops=1000000, moved=1000000, aliases=None, after=()):
    vmem = pl.BlockSpec(memory_space=pltpu.VMEM)
    smem = pl.BlockSpec(memory_space=pltpu.SMEM)
    held = len(args)

    def body(*refs):
        kernel(*refs[:held], *refs[held + len(after) :])

    return pl.pallas_call(
        body if after else kernel,
        out_shape=outs,
        in_specs=[smem] + [vmem] * (held - 1) + [pl.BlockSpec(memory_space=pl.ANY)] * len(after),
        out_specs=[vmem] * len(outs),
        scratch_shapes=list(scratch),
        input_output_aliases=aliases or {},
        compiler_params=pltpu.CompilerParams(vmem_limit_bytes=24 * 1024 * 1024),
        cost_estimate=pl.CostEstimate(flops=flops, bytes_accessed=moved, transcendentals=0),
    )(*args, *after)


def ring4(place, shift):
    return lax.bitwise_and(place + shift, 3)


def lanes(start, size):
    return pl.ds(pl.multiple_of(start * size, size), size)


def split3(vals):
    high = vals.astype(bf16)
    rest = vals - high.astype(f32)
    mid = rest.astype(bf16)
    low = (rest - mid.astype(f32)).astype(bf16)
    return high, mid, low


def iota(dims, dim):
    return lax.broadcasted_iota(jnp.int32, dims, dim)


def pack_kernel(decay, x, b, c, q, *outs):
    y = lax.bitwise_and(lax.axis_index("ctx").astype(jnp.int32), 3)
    lane = iota((LBLK, 128), 1)
    for s, out in enumerate(outs):
        j = ring4(y, s)
        group = lax.shift_right_logical(j, 1)
        out[:, 0:SLICE] = x[:, lanes(j, SLICE)]
        out[:, AT_B:AT_C] = b[:, lanes(group, NSTATE)]
        out[:, AT_C:AT_DECAY] = c[:, lanes(group, NSTATE)]
        high, mid, low = (part.astype(f32) for part in split3(decay[:, lanes(j, 128)]))
        out[:, AT_DECAY:AT_Q] = jnp.where(lane < 8, high, jnp.where(lane < 16, mid, low)).astype(bf16)
        out[:, AT_Q:] = q[:, lanes(lax.bitwise_and(j, 1), 4 * HDIM)]


def write_total(out, state, log_total):
    out[0:NSTATE, :] = state.astype(bf16)
    high, mid, low = split3(log_total)
    row = iota((16, log_total.shape[1]), 0)
    out[NSTATE:, :] = jnp.where(
        row == 0,
        high.astype(f32),
        jnp.where(row == 1, mid.astype(f32), jnp.where(row == 2, low.astype(f32), 0.0)),
    ).astype(bf16)


def read_total(vals):
    tail = vals[NSTATE:, :].astype(f32)
    return vals[0:NSTATE, :].astype(f32), tail[0:1] + tail[1:2] + tail[2:3]


def total_kernel(place, r0, r1, r2, r3, t0, t1, t2, t3, ordered, cums, states, total):
    x, y = place[1], place[2]
    for s, r in enumerate((r0, r1, r2, r3)):
        ordered[ring4(y, -s)] = r[:, :AT_Q]
    tri = (iota((LBLK, LBLK), 0) >= iota((LBLK, LBLK), 1)).astype(f32).astype(bf16)
    cum_parts = jnp.concatenate(
        [jnp.dot(tri, ordered[block, :, AT_DECAY:AT_Q], preferred_element_type=f32) for block in range(4)], axis=0
    )
    row = iota((128, SLICE), 0)
    head = lax.shift_right_logical(iota((128, SLICE), 1), 6)
    spread = jnp.where((lax.bitwise_and(row, 7) == head) & (row < 24), 1.0, 0.0).astype(bf16)
    cum_all = functools.reduce(
        jnp.add, [jnp.dot(part, spread, preferred_element_type=f32) for part in split3(cum_parts)]
    )
    log_total = jnp.zeros((1, SLICE), f32)
    for block in range(4):
        cum = cum_all[block * LBLK : (block + 1) * LBLK]
        last = cum[LBLK - 1 : LBLK, :]
        cums[block] = cum
        decayed = (ordered[block, :, 0:SLICE].astype(f32) * jnp.exp(last - cum)).astype(bf16)
        state = lax.dot_general(
            ordered[block, :, AT_B:AT_C], decayed, (((0,), (0,)), ((), ())), preferred_element_type=f32
        )
        states[block] = state
        log_total = log_total + last
        total[...] = state if block == 0 else jnp.exp(last) * total[...] + state
    for s, t in enumerate((t0, t1, t2, t3)):
        j = ring4(x, s)
        log_part = jnp.where(
            j == 0,
            log_total[:, 0:128],
            jnp.where(j == 1, log_total[:, 128:256], jnp.where(j == 2, log_total[:, 256:384], log_total[:, 384:512])),
        )
        write_total(t, total[:, lanes(j, 128)], log_part)


def local_kernel(place, ordered, cums, states, skip, local, decay, held):
    gain = skip[:, lanes(place[2], SLICE)]
    causal = iota((LBLK, LBLK), 0) >= iota((LBLK, LBLK), 1)
    tri = causal.astype(f32).astype(bf16)
    low_half = iota((LBLK, 128), 1) < MHDIM
    before = jnp.zeros((1, SLICE), f32)
    for block in range(4):
        cum = cums[block]
        last = cum[LBLK - 1 : LBLK, :]
        decay[block] = jnp.exp(cum + before)
        before = before + last
        parts = ordered[block, :, AT_DECAY:AT_Q]
        row_parts = lax.dot_general(parts, tri, (((0,), (1,)), ((), ())), preferred_element_type=f32)
        cum_rows = row_parts[0:8] + row_parts[8:16] + row_parts[16:24]
        read = ordered[block, :, AT_C:AT_DECAY]
        pair_dots = lax.dot_general(
            read, ordered[block, :, AT_B:AT_C], (((1,), (1,)), ((), ())), preferred_element_type=f32
        )
        if block == 0:
            held[...] = states[0]
        else:
            state = held[...]
            high = state.astype(bf16)
            low = (state - high.astype(f32)).astype(bf16)
            inflow = jnp.dot(read, high, preferred_element_type=f32) + jnp.dot(read, low, preferred_element_type=f32)
            if block < 3:
                held[...] = jnp.exp(last) * state + states[block]
        for pair in range(4):
            part = slice(pair * 128, pair * 128 + 128)
            xs = ordered[block, :, part]
            sums = []
            for head in (2 * pair, 2 * pair + 1):
                gap = cum[:, head * MHDIM : head * MHDIM + 1] - cum_rows[head : head + 1, :]
                weight = (jnp.exp(jnp.where(causal, gap, neg_large)) * pair_dots).astype(bf16)
                sums.append(jnp.dot(weight, xs, preferred_element_type=f32))
            vals = jnp.where(low_half, sums[0], sums[1]) + gain[:, part] * xs.astype(f32)
            if block > 0:
                vals = vals + jnp.exp(cum[:, part]) * inflow[:, part]
            local[block, :, part] = vals


def plane_kernel(place, r0, r1, r2, r3, out, ordered):
    x = place[1]
    for s, r in enumerate((r0, r1, r2, r3)):
        ordered[ring4(x, -s)] = r[...]
    total, log_total = read_total(ordered[0])
    for block in range(1, 4):
        state, last = read_total(ordered[block])
        total = jnp.exp(last) * total + state
        log_total = log_total + last
    write_total(out, total, log_total)


def entering_kernel(place, r0, r1, r2, r3, up1, up2, up3, g0, g1, g2, g3, ordered, entering):
    x = place[1]
    for s, r in enumerate((r0, r1, r2, r3)):
        ordered[ring4(x, -s)] = r[...]
    current, _ = read_total(up3[...])
    for up in (up2, up1):
        state, last = read_total(up[...])
        current = jnp.exp(last) * current + state
    for block in range(4):
        entering[block] = current.astype(bf16)
        if block < 3:
            state, last = read_total(ordered[block])
            current = jnp.exp(last) * current + state
    for s, g in enumerate((g0, g1, g2, g3)):
        g[...] = entering[ring4(x, s)]


def mixed_kernel(place, ordered, local, decay, g0, g1, g2, g3, m0, m1, m2, m3, carried, results):
    x, y = place[1], place[2]
    for s, g in enumerate((g0, g1, g2, g3)):
        carried[:, lanes(ring4(x, -s), 128)] = g[...]
    for block in range(4):
        inflow = jnp.dot(ordered[block, :, AT_C:AT_DECAY], carried[...], preferred_element_type=f32)
        results[block] = (local[block] + decay[block] * inflow).astype(bf16)
    for s, m in enumerate((m0, m1, m2, m3)):
        m[...] = results[ring4(y, s)]


def silu_kernel(place, gate, out):
    gates = gate[...].astype(f32)
    out[...] = gates / (1.0 + jnp.exp(-gates))


def norm_kernel(place, m0, m1, m2, m3, gates, gain, out):
    y = place[2]
    gated, squares, groups, slots = [], [], [], []
    for s, m in enumerate((m0, m1, m2, m3)):
        j = ring4(y, -s)
        vals = m[...].astype(f32) * gates[:, lanes(j, SLICE)]
        gated.append(vals)
        squares.append(jnp.sum(vals * vals, axis=1, keepdims=True))
        groups.append(lax.shift_right_logical(j, 1))
        slots.append(j)
    for s in range(4):
        total = jnp.zeros((LBLK, 1), f32)
        for other in range(4):
            total = total + jnp.where(groups[other] == groups[s], squares[other], 0.0)
        factor = lax.rsqrt(total * (1.0 / 1024.0) + eps_norm)
        out[:, lanes(slots[s], SLICE)] = (gated[s] * factor * gain[:, lanes(slots[s], SLICE)]).astype(bf16)


def query_tile(rings, tile):
    head = tile % 4
    return rings[tile // 4][:, AT_Q + head * HDIM : AT_Q + (head + 1) * HDIM]


def with_ones(value):
    return jnp.concatenate([value, jnp.ones_like(value)], axis=1)


def attend(tile, queries, keys, values, state, limit=None):
    tops, sums, acc = state
    rows = slice(tile * LBLK, (tile + 1) * LBLK)
    scores = [
        lax.dot_general(queries, key, (((1,), (1,)), ((), ())), preferred_element_type=f32) for key in keys
    ]
    if limit is not None:
        scores = limit(scores)
    top = functools.reduce(jnp.maximum, scores)
    held_top = tops[rows, 0:1]
    new_top = jnp.maximum(held_top, jnp.max(top, axis=1, keepdims=True))
    expos = [jnp.exp2((score - new_top) * score_scale).astype(bf16) for score in scores]
    factor = jnp.exp2((held_top - new_top) * score_scale)
    summed = functools.reduce(
        jnp.add, [jnp.dot(expo, value, preferred_element_type=f32) for expo, value in zip(expos, values)]
    )
    tops[rows, :] = jnp.broadcast_to(new_top, (LBLK, 128))
    sums[rows, :] = sums[rows, :] * factor + summed[:, HDIM:]
    acc[rows, :] = acc[rows, :] * factor + summed[:, :HDIM]


def plane_offsets(place, column):
    earlier = [column < place[1]] + [place[0] >= distance for distance in (1, 2, 3)]
    return [jnp.where(one, 0.0, neg_large).astype(f32) for one in earlier]


def add_offsets(scores, offsets):
    return [score + offset for score, offset in zip(scores, offsets)]


def own_kernel(place, r0, r1, r2, r3, kv0, kv1, kv2, kv3, tops, sums, acc):
    y = place[2]
    tops[...] = jnp.full(tops.shape, no_top, f32)
    sums[...] = jnp.zeros(sums.shape, f32)
    acc[...] = jnp.zeros(acc.shape, f32)
    blocks = (kv0, kv1, kv2, kv3)
    keys = [kv[:, :HDIM] for kv in blocks]
    values = [with_ones(kv[:, HDIM:]) for kv in blocks]
    lane = iota((LBLK, KVW), 1)
    key_pos = jnp.where(lane < LBLK, y * LBLK, lax.bitwise_xor(y, 1) * LBLK) + lax.bitwise_and(lane, LBLK - 1)
    ahead = key_pos - iota((LBLK, KVW), 0)
    offsets = plane_offsets(place, 0)[1:]

    def all_tiles(offsets):
        for tile in range(16):
            first = ring4(y, -(tile // 4)) * LBLK

            def limit(scores, first=first):
                later = scores[1:] if offsets is None else add_offsets(scores[1:], offsets)
                return [jnp.where(ahead <= first, scores[0], neg_large)] + later

            attend(tile, query_tile((r0, r1, r2, r3), tile), keys, values, (tops, sums, acc), limit)

    pl.when(place[0] >= 3)(lambda: all_tiles(None))
    pl.when(place[0] < 3)(lambda: all_tiles(offsets))


def column_attend(step, place, r0, r1, r2, r3, old_tops, old_sums, old_acc, *refs):
    columns = refs[: (2 if step == 2 else 1)]
    outs = refs[len(columns) :]
    state = outs[:3]
    other = ring4(place[1], step)
    offsets = plane_offsets(place, other)
    size = columns[0].shape[0] // KVW
    blocks = [columns[block // size][block % size * KVW : (block % size + 1) * KVW, :] for block in range(4)]
    keys = [kv[:, :HDIM] for kv in blocks]
    values = [with_ones(kv[:, HDIM:]) for kv in blocks]

    def all_tiles(first, offsets):
        limit = None if offsets is None else functools.partial(add_offsets, offsets=offsets)
        for tile in range(16):
            attend(tile, query_tile((r0, r1, r2, r3), tile), keys[first:], values[first:], state, limit)

    top_plane = place[0] >= 3
    pl.when(top_plane & (other < place[1]))(lambda: all_tiles(0, None))
    pl.when(top_plane & (other >= place[1]))(lambda: all_tiles(1, None))
    pl.when(place[0] < 3)(lambda: all_tiles(0, offsets))
    if step == 2:
        tops, sums, acc = state
        lane = iota((LBLK, 128), 1)
        for s, o in enumerate(outs[3:]):
            stats = jnp.zeros((LBLK, 128), f32)
            for head in range(4):
                start = (s * 4 + head) * LBLK
                rows = slice(start, start + LBLK)
                total = sums[rows, :]
                o[:, head * HDIM : (head + 1) * HDIM] = (acc[rows, :] / jnp.where(total > 0, total, 1.0)).astype(bf16)
                stats = jnp.where(lane == head * 6, tops[rows, :], jnp.where(lane == head * 6 + 3, total, stats))
            high, mid, low = (part.astype(f32) for part in split3(stats))
            o[:, 4 * HDIM :] = (high + pltpu.roll(mid, 1, 1) + pltpu.roll(low, 2, 1)).astype(bf16)


def merge_kernel(place, o0, o1, o2, o3, out):
    head_group = lax.bitwise_and(place[2], 1)
    for pair, group in (((o0, o2), head_group), ((o1, o3), 1 - head_group)):
        tops, sums = [], []
        for part in pair:
            stats = part[:, 4 * HDIM :].astype(f32)
            stats = stats + pltpu.roll(stats, 127, 1) + pltpu.roll(stats, 126, 1)
            tops.append(stats)
            sums.append(pltpu.roll(stats, 125, 1))
        top = jnp.maximum(tops[0], tops[1])
        weights = [total * jnp.exp2(jnp.minimum((one - top) * score_scale, 0.0)) for one, total in zip(tops, sums)]
        whole = weights[0] + weights[1]
        shares = [weight / jnp.where(whole > 0, whole, 1.0) for weight in weights]
        for head in range(4):
            cols = slice(head * HDIM, (head + 1) * HDIM)
            vals = [
                part[:, cols].astype(f32) * share[:, head * 6 : head * 6 + 1] for part, share in zip(pair, shares)
            ]
            start = pl.multiple_of(group * (4 * HDIM) + head * HDIM, HDIM)
            out[:, pl.ds(start, HDIM)] = (vals[0] + vals[1]).astype(bf16)


def shift_y(vals, shift):
    return lax.ppermute(vals, "ctx", [(i, (i & ~3) | ((i + shift) & 3)) for i in range(64)])


def shift_x(vals, shift):
    return lax.ppermute(vals, "ctx", [(i, (i & ~12) | ((i + 4 * shift) & 12)) for i in range(64)])


def up_z(vals, shift):
    return lax.ppermute(vals, "ctx", [(i, i + 16 * shift) for i in range(64 - 16 * shift)])


def on_device(
    step_inputs, log_decay, write_vecs, read_vecs, gate_vals, skip_gain, norm_gain, query_rows, key_rows, value_rows
):
    index = lax.axis_index("ctx").astype(jnp.int32)
    place = jnp.stack([index // 16, (index // 4) % 4, index % 4, index])
    decay_copies = jnp.tile(log_decay.reshape(LBLK, 4, 1, 8), (1, 1, 3, 1)).reshape(LBLK, 4, 24)
    decay_grid = jnp.pad(decay_copies, ((0, 0), (0, 0), (0, 104))).reshape(LBLK, 512)
    skip = jnp.repeat(skip_gain, MHDIM).reshape(1, 4 * SLICE)
    gain = norm_gain.reshape(1, 4 * SLICE)

    head = (index % 2) * HDIM

    def one_head(start):
        parts = [lax.dynamic_slice_in_dim(rows, start, HDIM, 1) for rows in (key_rows, value_rows)]
        return jnp.concatenate(parts, axis=1)

    kv_own, kv_other = one_head(head), one_head(HDIM - head)
    kv_recv = lax.ppermute(kv_other, "ctx", [(i, i ^ 1) for i in range(64)])
    vmem = pl.BlockSpec(memory_space=pltpu.VMEM)
    rings = pl.pallas_call(
        pack_kernel,
        out_shape=[shape((LBLK, WIDTH), bf16)] * 4,
        in_specs=[vmem] * 5,
        out_specs=[vmem] * 4,
        compiler_params=pltpu.CompilerParams(vmem_limit_bytes=60 * 1024 * 1024),
    )(decay_grid, step_inputs, write_vecs, read_vecs, query_rows)
    rings = [rings[0]] + [shift_y(rings[s], s) for s in (1, 2, 3)]

    kv = jnp.concatenate([kv_own, kv_recv], axis=0)
    up1, up2 = up_z(kv, 1), up_z(kv, 2)
    ups = [up1, up2, up_z(up2, 1)]
    column = jnp.concatenate([kv] + ups, axis=0)
    left, right = shift_x(column, 1), shift_x(column, -1)
    half = 2 * KVW
    opposite = [shift_x(left[:half], 1), shift_x(right[half:], -1)]

    gates = run(silu_kernel, [shape((LBLK, 4 * SLICE), f32)], (place, gate_vals), moved=2 << 20)[0]
    ring_grid = [shape((4, LBLK, SLICE), f32)] * 2
    *totals, ordered, cums, states = run(
        total_kernel,
        [shape((NSTATE + 16, 128), bf16)] * 4
        + [shape((4, LBLK, AT_Q), bf16), ring_grid[0], shape((4, NSTATE, SLICE), f32)],
        (place, *rings),
        [pltpu.VMEM((NSTATE, SLICE), f32)],
        flops=600 << 20,
        moved=2 << 20,
        after=[ups[2], gates],
    )
    totals = [totals[0]] + [shift_x(totals[s], s) for s in (1, 2, 3)]

    rows = 16 * LBLK
    state_shapes = [shape((rows, 128), f32)] * 3
    out_shapes = [shape((LBLK, 4 * HDIM + 128), bf16)] * 4

    def attend_column(state, step, keys, after=()):
        return run(
            functools.partial(column_attend, step),
            state_shapes + (out_shapes if step == 2 else []),
            (place, *rings, *state, *keys),
            flops=4 << 30,
            moved=8 << 20,
            aliases={5: 0, 6: 1, 7: 2},
            after=after,
        )

    state = run(own_kernel, state_shapes, (place, *rings, kv, *ups), flops=4 << 30, moved=8 << 20, after=[totals[0]])
    (plane_total,) = run(
        plane_kernel,
        [shape((NSTATE + 16, 128), bf16)],
        (place, *totals),
        [pltpu.VMEM((4, NSTATE + 16, 128), bf16)],
        after=[state[1]],
    )
    total_ups = [up_z(plane_total, s) for s in (1, 2, 3)]
    state = attend_column(state, -1, [left], [plane_total])
    entering = run(
        entering_kernel,
        [shape((NSTATE, 128), bf16)] * 4,
        (place, *totals, *total_ups),
        [pltpu.VMEM((4, NSTATE + 16, 128), bf16), pltpu.VMEM((4, NSTATE, 128), bf16)],
        after=[state[1]],
    )
    local, decay = run(
        local_kernel,
        ring_grid,
        (place, ordered, cums, states, skip),
        [pltpu.VMEM((NSTATE, SLICE), f32)],
        flops=2 << 30,
        moved=4 << 20,
        after=[entering[0]],
    )
    entering = [entering[0]] + [shift_x(entering[s], s) for s in (1, 2, 3)]
    mixed = run(
        mixed_kernel,
        [shape((LBLK, SLICE), bf16)] * 4,
        (place, ordered, local, decay, *entering),
        [pltpu.VMEM((NSTATE, SLICE), bf16), pltpu.VMEM((4, LBLK, SLICE), bf16)],
    )
    state = attend_column(state, 1, [right], [mixed[0]])
    mixed = [mixed[0]] + [shift_y(mixed[s], s) for s in (1, 2, 3)]
    *_, o0, o1, o2, o3 = attend_column(state, 2, opposite, mixed[1:])
    outs = [o0] + [shift_y(one, -s) for s, one in ((1, o1), (2, o2), (3, o3))]
    (mamba_out,) = run(norm_kernel, [shape((LBLK, 4 * SLICE), bf16)], (place, *mixed, gates, gain), after=[o0])
    (attn_out,) = run(merge_kernel, [shape((LBLK, 8 * HDIM), bf16)], (place, *outs))
    return (mamba_out, attn_out)


def solution(mesh):
    in_specs = (
        P("ctx", "tp"),
        P("ctx", "tp"),
        P("ctx", "tp"),
        P("ctx", "tp"),
        P("ctx", "tp"),
        P("tp"),
        P("tp"),
        P("ctx", "tp"),
        P("ctx", "tp"),
        P("ctx", "tp"),
    )
    out_specs = (P("ctx", "tp"), P("ctx", "tp"))
    return jax.shard_map(on_device, mesh=mesh, in_specs=in_specs, out_specs=out_specs, check_vma=False)
```

```python
import functools

import jax
import jax.numpy as jnp
from jax import lax
from jax.experimental import pallas as pl
from jax.experimental.pallas import tpu as pltpu
from jax.sharding import PartitionSpec as P

MHDIM = 64
NSTATE = 256
HDIM = 128
LBLK = 128
SLICE = 512
KVW = 2 * HDIM
AT_B = SLICE
AT_C = AT_B + NSTATE
AT_DECAY = AT_C + NSTATE
WIDTH = AT_DECAY + 128

eps_norm = 1e-05
neg_large = -1e30
no_top = -1e29
score_scale = HDIM ** (-0.5) * 1.4426950408889634

bf16 = jnp.bfloat16
f32 = jnp.float32


def shape(dims, dtype):
    return jax.ShapeDtypeStruct(dims, dtype)


def run(kernel, outs, args, scratch=(), flops=1000000, moved=1000000, aliases=None, after=()):
    vmem = pl.BlockSpec(memory_space=pltpu.VMEM)
    smem = pl.BlockSpec(memory_space=pltpu.SMEM)
    held = len(args)

    def body(*refs):
        kernel(*refs[:held], *refs[held + len(after) :])

    return pl.pallas_call(
        body if after else kernel,
        out_shape=outs,
        in_specs=[smem] + [vmem] * (held - 1) + [pl.BlockSpec(memory_space=pl.ANY)] * len(after),
        out_specs=[vmem] * len(outs),
        scratch_shapes=list(scratch),
        input_output_aliases=aliases or {},
        compiler_params=pltpu.CompilerParams(vmem_limit_bytes=24 * 1024 * 1024),
        cost_estimate=pl.CostEstimate(flops=flops, bytes_accessed=moved, transcendentals=0),
    )(*args, *after)


def ring4(place, shift):
    return lax.bitwise_and(place + shift, 3)


def lanes(start, size):
    return pl.ds(pl.multiple_of(start * size, size), size)


def split3(vals):
    high = vals.astype(bf16)
    rest = vals - high.astype(f32)
    mid = rest.astype(bf16)
    low = (rest - mid.astype(f32)).astype(bf16)
    return high, mid, low


def iota(dims, dim):
    return lax.broadcasted_iota(jnp.int32, dims, dim)


def pack_kernel(decay, x, b, c, *outs):
    y = lax.bitwise_and(lax.axis_index("ctx").astype(jnp.int32), 3)
    lane = iota((LBLK, 128), 1)
    for s, out in enumerate(outs):
        j = ring4(y, s)
        group = lax.shift_right_logical(j, 1)
        out[:, 0:SLICE] = x[:, lanes(j, SLICE)]
        out[:, AT_B:AT_C] = b[:, lanes(group, NSTATE)]
        out[:, AT_C:AT_DECAY] = c[:, lanes(group, NSTATE)]
        high, mid, low = (part.astype(f32) for part in split3(decay[:, lanes(j, 128)]))
        out[:, AT_DECAY:] = jnp.where(lane < 8, high, jnp.where(lane < 16, mid, low)).astype(bf16)


def pair_kernel(place, own, swapped, out):
    out[0:LBLK, :] = own[...]
    out[LBLK:, :] = swapped[:, :KVW]


def write_total(out, state, log_total):
    out[0:NSTATE, :] = state.astype(bf16)
    high, mid, low = split3(log_total)
    row = iota((16, log_total.shape[1]), 0)
    out[NSTATE:, :] = jnp.where(
        row == 0,
        high.astype(f32),
        jnp.where(row == 1, mid.astype(f32), jnp.where(row == 2, low.astype(f32), 0.0)),
    ).astype(bf16)


def read_total(vals):
    tail = vals[NSTATE:, :].astype(f32)
    return vals[0:NSTATE, :].astype(f32), tail[0:1] + tail[1:2] + tail[2:3]


def total_kernel(place, r0, r1, r2, r3, t0, t1, t2, t3, ordered, cums, states, total):
    x, y = place[1], place[2]
    for s, r in enumerate((r0, r1, r2, r3)):
        ordered[ring4(y, -s)] = r[...]
    tri = (iota((LBLK, LBLK), 0) >= iota((LBLK, LBLK), 1)).astype(f32).astype(bf16)
    cum_parts = jnp.concatenate(
        [jnp.dot(tri, ordered[block, :, AT_DECAY:], preferred_element_type=f32) for block in range(4)], axis=0
    )
    row = iota((128, SLICE), 0)
    head = lax.shift_right_logical(iota((128, SLICE), 1), 6)
    spread = jnp.where((lax.bitwise_and(row, 7) == head) & (row < 24), 1.0, 0.0).astype(bf16)
    cum_all = functools.reduce(
        jnp.add, [jnp.dot(part, spread, preferred_element_type=f32) for part in split3(cum_parts)]
    )
    log_total = jnp.zeros((1, SLICE), f32)
    for block in range(4):
        cum = cum_all[block * LBLK : (block + 1) * LBLK]
        last = cum[LBLK - 1 : LBLK, :]
        cums[block] = cum
        decayed = (ordered[block, :, 0:SLICE].astype(f32) * jnp.exp(last - cum)).astype(bf16)
        state = lax.dot_general(
            ordered[block, :, AT_B:AT_C], decayed, (((0,), (0,)), ((), ())), preferred_element_type=f32
        )
        states[block] = state
        log_total = log_total + last
        total[...] = state if block == 0 else jnp.exp(last) * total[...] + state
    for s, t in enumerate((t0, t1, t2, t3)):
        j = ring4(x, s)
        log_part = jnp.where(
            j == 0,
            log_total[:, 0:128],
            jnp.where(j == 1, log_total[:, 128:256], jnp.where(j == 2, log_total[:, 256:384], log_total[:, 384:512])),
        )
        write_total(t, total[:, lanes(j, 128)], log_part)


def local_kernel(place, ordered, cums, states, skip, local, decay, held):
    gain = skip[:, lanes(place[2], SLICE)]
    causal = iota((LBLK, LBLK), 0) >= iota((LBLK, LBLK), 1)
    tri = causal.astype(f32).astype(bf16)
    low_half = iota((LBLK, 128), 1) < MHDIM
    before = jnp.zeros((1, SLICE), f32)
    for block in range(4):
        cum = cums[block]
        last = cum[LBLK - 1 : LBLK, :]
        decay[block] = jnp.exp(cum + before)
        before = before + last
        parts = ordered[block, :, AT_DECAY:]
        row_parts = lax.dot_general(parts, tri, (((0,), (1,)), ((), ())), preferred_element_type=f32)
        cum_rows = row_parts[0:8] + row_parts[8:16] + row_parts[16:24]
        read = ordered[block, :, AT_C:AT_DECAY]
        pair_dots = lax.dot_general(
            read, ordered[block, :, AT_B:AT_C], (((1,), (1,)), ((), ())), preferred_element_type=f32
        )
        if block == 0:
            held[...] = states[0]
        else:
            state = held[...]
            high = state.astype(bf16)
            low = (state - high.astype(f32)).astype(bf16)
            inflow = jnp.dot(read, high, preferred_element_type=f32) + jnp.dot(read, low, preferred_element_type=f32)
            if block < 3:
                held[...] = jnp.exp(last) * state + states[block]
        for pair in range(4):
            part = slice(pair * 128, pair * 128 + 128)
            xs = ordered[block, :, part]
            sums = []
            for head in (2 * pair, 2 * pair + 1):
                gap = cum[:, head * MHDIM : head * MHDIM + 1] - cum_rows[head : head + 1, :]
                weight = (jnp.exp(jnp.where(causal, gap, neg_large)) * pair_dots).astype(bf16)
                sums.append(jnp.dot(weight, xs, preferred_element_type=f32))
            vals = jnp.where(low_half, sums[0], sums[1]) + gain[:, part] * xs.astype(f32)
            if block > 0:
                vals = vals + jnp.exp(cum[:, part]) * inflow[:, part]
            local[block, :, part] = vals


def plane_kernel(place, r0, r1, r2, r3, out, ordered):
    x = place[1]
    for s, r in enumerate((r0, r1, r2, r3)):
        ordered[ring4(x, -s)] = r[...]
    total, log_total = read_total(ordered[0])
    for block in range(1, 4):
        state, last = read_total(ordered[block])
        total = jnp.exp(last) * total + state
        log_total = log_total + last
    write_total(out, total, log_total)


def entering_kernel(place, r0, r1, r2, r3, up1, up2, up3, g0, g1, g2, g3, ordered, entering):
    x = place[1]
    for s, r in enumerate((r0, r1, r2, r3)):
        ordered[ring4(x, -s)] = r[...]
    current = jnp.zeros((NSTATE, 128), f32)
    for distance, up in ((3, up3), (2, up2), (1, up1)):
        state, last = read_total(up[...])
        current = jnp.where(place[0] >= distance, jnp.exp(last) * current + state, 0.0)
    for block in range(4):
        entering[block] = current.astype(bf16)
        if block < 3:
            state, last = read_total(ordered[block])
            current = jnp.exp(last) * current + state
    for s, g in enumerate((g0, g1, g2, g3)):
        g[...] = entering[ring4(x, s)]


def mixed_kernel(place, ordered, local, decay, g0, g1, g2, g3, m0, m1, m2, m3, carried, results):
    x, y = place[1], place[2]
    for s, g in enumerate((g0, g1, g2, g3)):
        carried[:, lanes(ring4(x, -s), 128)] = g[...]
    for block in range(4):
        inflow = jnp.dot(ordered[block, :, AT_C:AT_DECAY], carried[...], preferred_element_type=f32)
        results[block] = (local[block] + decay[block] * inflow).astype(bf16)
    for s, m in enumerate((m0, m1, m2, m3)):
        m[...] = results[ring4(y, s)]


def silu_kernel(place, gate, out):
    gates = gate[...].astype(f32)
    out[...] = gates / (1.0 + jnp.exp(-gates))


def norm_kernel(place, m0, m1, m2, m3, gates, gain, out):
    y = place[2]
    gated, squares, groups, slots = [], [], [], []
    for s, m in enumerate((m0, m1, m2, m3)):
        j = ring4(y, -s)
        vals = m[...].astype(f32) * gates[:, lanes(j, SLICE)]
        gated.append(vals)
        squares.append(jnp.sum(vals * vals, axis=1, keepdims=True))
        groups.append(lax.shift_right_logical(j, 1))
        slots.append(j)
    for s in range(4):
        total = jnp.zeros((LBLK, 1), f32)
        for other in range(4):
            total = total + jnp.where(groups[other] == groups[s], squares[other], 0.0)
        factor = lax.rsqrt(total * (1.0 / 1024.0) + eps_norm)
        out[:, lanes(slots[s], SLICE)] = (gated[s] * factor * gain[:, lanes(slots[s], SLICE)]).astype(bf16)


def query_tile(queries, tile):
    one, head = queries[tile // 4], tile % 4
    start = one.shape[1] - (4 - head) * HDIM
    return one[:, start : start + HDIM]


def with_ones(value):
    return jnp.concatenate([value, jnp.ones_like(value)], axis=1)


def attend(tile, queries, keys, values, state, limit=None):
    tops, sums, acc = state
    rows = slice(tile * LBLK, (tile + 1) * LBLK)
    scores = [
        lax.dot_general(queries, key, (((1,), (1,)), ((), ())), preferred_element_type=f32) for key in keys
    ]
    if limit is not None:
        scores = limit(scores)
    top = functools.reduce(jnp.maximum, scores)
    held_top = tops[rows, 0:1]
    new_top = jnp.maximum(held_top, jnp.max(top, axis=1, keepdims=True))
    expos = [jnp.exp2((score - new_top) * score_scale).astype(bf16) for score in scores]
    factor = jnp.exp2((held_top - new_top) * score_scale)
    summed = functools.reduce(
        jnp.add, [jnp.dot(expo, value, preferred_element_type=f32) for expo, value in zip(expos, values)]
    )
    tops[rows, :] = jnp.broadcast_to(new_top, (LBLK, 128))
    sums[rows, :] = sums[rows, :] * factor + summed[:, HDIM:]
    acc[rows, :] = acc[rows, :] * factor + summed[:, :HDIM]


def offset(visible):
    return jnp.where(visible, 0.0, neg_large).astype(f32)


def add_offsets(scores, offsets):
    return [score if one is None else score + one for score, one in zip(scores, offsets)]


def every_tile(place, queries, keys, values, state, own_plane):
    def all_tiles(offsets):
        for tile in range(16):

            def limit(scores, slot=tile // 4):
                return [own_plane(scores[0], slot)] + add_offsets(scores[1:], offsets)

            attend(tile, query_tile(queries, tile), keys, values, state, limit)

    pl.when(place[0] >= 3)(lambda: all_tiles([None] * 3))
    pl.when(place[0] < 3)(lambda: all_tiles([offset(place[0] >= distance) for distance in (1, 2, 3)]))


def own_kernel(place, q0, q1, q2, q3, kv0, kv1, kv2, kv3, tops, sums, acc):
    x = place[1]
    tops[...] = jnp.full(tops.shape, no_top, f32)
    sums[...] = jnp.zeros(sums.shape, f32)
    acc[...] = jnp.zeros(acc.shape, f32)
    blocks = (kv0, kv1, kv2, kv3)
    keys = [kv[:, :HDIM] for kv in blocks]
    values = [with_ones(kv[:, HDIM:]) for kv in blocks]
    lane = iota((LBLK, KVW), 1)
    key_pos = jnp.where(lane < LBLK, x, lax.bitwise_xor(x, 1)) * LBLK + lax.bitwise_and(lane, LBLK - 1)
    ahead = key_pos - iota((LBLK, KVW), 0)

    def own_plane(score, slot):
        return jnp.where(ahead <= lax.bitwise_xor(x, slot) * LBLK, score, neg_large)

    every_tile(place, (q0, q1, q2, q3), keys, values, (tops, sums, acc), own_plane)


def column_attend(step, place, q0, q1, q2, q3, old_tops, old_sums, old_acc, *refs):
    columns = refs[: (2 if step == 2 else 1)]
    outs = refs[len(columns) :]
    state = outs[:3]
    x, y = place[1], place[2]
    other = ring4(y, step)
    size = columns[0].shape[0] // KVW
    blocks = [columns[block // size][block % size * KVW : (block % size + 1) * KVW, :] for block in range(4)]
    keys = [kv[:, :HDIM] for kv in blocks]
    values = [with_ones(kv[:, HDIM:]) for kv in blocks]
    lane = iota((1, KVW), 1)

    def own_plane(score, slot):
        query_block = lax.bitwise_xor(x, slot) * 4 + y
        near, far = (offset(one * 4 + other < query_block) for one in (x, lax.bitwise_xor(x, 1)))
        return score + jnp.where(lane < LBLK, near, far)

    every_tile(place, (q0, q1, q2, q3), keys, values, state, own_plane)
    if step == 2:
        tops, sums, acc = state
        lane = iota((LBLK, 128), 1)
        for s, o in enumerate(outs[3:]):
            stats = jnp.zeros((LBLK, 128), f32)
            for head in range(4):
                start = (s * 4 + head) * LBLK
                rows = slice(start, start + LBLK)
                total = sums[rows, :]
                o[:, head * HDIM : (head + 1) * HDIM] = (acc[rows, :] / jnp.where(total > 0, total, 1.0)).astype(bf16)
                stats = jnp.where(lane == head * 6, tops[rows, :], jnp.where(lane == head * 6 + 3, total, stats))
            high, mid, low = (part.astype(f32) for part in split3(stats))
            o[:, 4 * HDIM :] = (high + pltpu.roll(mid, 1, 1) + pltpu.roll(low, 2, 1)).astype(bf16)


def merge_kernel(place, o0, o1, o2, o3, out):
    head_group = lax.bitwise_and(place[1], 1)
    for pair, group in (((o0, o2), head_group), ((o1, o3), 1 - head_group)):
        tops, sums = [], []
        for part in pair:
            stats = part[:, 4 * HDIM :].astype(f32)
            stats = stats + pltpu.roll(stats, 127, 1) + pltpu.roll(stats, 126, 1)
            tops.append(stats)
            sums.append(pltpu.roll(stats, 125, 1))
        top = jnp.maximum(tops[0], tops[1])
        weights = [total * jnp.exp2(jnp.minimum((one - top) * score_scale, 0.0)) for one, total in zip(tops, sums)]
        whole = weights[0] + weights[1]
        shares = [weight / jnp.where(whole > 0, whole, 1.0) for weight in weights]
        for head in range(4):
            cols = slice(head * HDIM, (head + 1) * HDIM)
            vals = [
                part[:, cols].astype(f32) * share[:, head * 6 : head * 6 + 1] for part, share in zip(pair, shares)
            ]
            start = pl.multiple_of(group * (4 * HDIM) + head * HDIM, HDIM)
            out[:, pl.ds(start, HDIM)] = (vals[0] + vals[1]).astype(bf16)


def shift_y(vals, shift):
    return lax.ppermute(vals, "ctx", [(i, (i & ~3) | ((i + shift) & 3)) for i in range(64)])


def shift_x(vals, shift):
    return lax.ppermute(vals, "ctx", [(i, (i & ~12) | ((i + 4 * shift) & 12)) for i in range(64)])


def swap_x(vals, step):
    return lax.ppermute(vals, "ctx", [(i, i ^ (4 * step)) for i in range(64)])


def up_z(vals, shift):
    return lax.ppermute(vals, "ctx", [(i, (i + 16 * shift) & 63) for i in range(64)])


def on_device(
    step_inputs, log_decay, write_vecs, read_vecs, gate_vals, skip_gain, norm_gain, query_rows, key_rows, value_rows
):
    index = lax.axis_index("ctx").astype(jnp.int32)
    place = jnp.stack([index // 16, (index // 4) % 4, index % 4, index])
    decay_copies = jnp.tile(log_decay.reshape(LBLK, 4, 1, 8), (1, 1, 3, 1)).reshape(LBLK, 4, 24)
    decay_grid = jnp.pad(decay_copies, ((0, 0), (0, 0), (0, 104))).reshape(LBLK, 512)
    skip = jnp.repeat(skip_gain, MHDIM).reshape(1, 4 * SLICE)
    gain = norm_gain.reshape(1, 4 * SLICE)

    head = (index // 4) % 2

    def one_head(group):
        parts = [lax.dynamic_slice_in_dim(rows, group * HDIM, HDIM, 1) for rows in (key_rows, value_rows)]
        return jnp.concatenate(parts, axis=1)

    def its_queries(group):
        return lax.dynamic_slice_in_dim(query_rows, group * (4 * HDIM), 4 * HDIM, 1)

    kv_own, q_same, q_other = one_head(head), its_queries(head), its_queries(1 - head)
    swapped = swap_x(jnp.concatenate([one_head(1 - head), q_other], axis=1), 1)
    vmem = pl.BlockSpec(memory_space=pltpu.VMEM)
    rings = pl.pallas_call(
        pack_kernel,
        out_shape=[shape((LBLK, WIDTH), bf16)] * 4,
        in_specs=[vmem] * 4,
        out_specs=[vmem] * 4,
        compiler_params=pltpu.CompilerParams(vmem_limit_bytes=60 * 1024 * 1024),
    )(decay_grid, step_inputs, write_vecs, read_vecs)
    rings = [rings[0]] + [shift_y(rings[s], s) for s in (1, 2, 3)]

    queries = [q_same, swapped, swap_x(q_same, 2), swap_x(q_other, 3)]

    (kv,) = run(pair_kernel, [shape((2 * LBLK, KVW), bf16)], (place, kv_own, swapped), after=[rings[0]])
    up1, up2 = up_z(kv, 1), up_z(kv, 2)
    ups = [up1, up2, up_z(up2, 1)]
    column = jnp.concatenate([kv] + ups, axis=0)
    left, right = shift_y(column, 1), shift_y(column, -1)
    half = 2 * KVW
    opposite = [shift_y(left[:half], 1), shift_y(right[half:], -1)]

    gates = run(silu_kernel, [shape((LBLK, 4 * SLICE), f32)], (place, gate_vals), moved=2 << 20)[0]
    ring_grid = [shape((4, LBLK, SLICE), f32)] * 2
    *totals, ordered, cums, states = run(
        total_kernel,
        [shape((NSTATE + 16, 128), bf16)] * 4
        + [shape((4, LBLK, WIDTH), bf16), ring_grid[0], shape((4, NSTATE, SLICE), f32)],
        (place, *rings),
        [pltpu.VMEM((NSTATE, SLICE), f32)],
        flops=600 << 20,
        moved=2 << 20,
        after=[ups[2], gates],
    )
    totals = [totals[0]] + [shift_x(totals[s], s) for s in (1, 2, 3)]

    rows = 16 * LBLK
    state_shapes = [shape((rows, 128), f32)] * 3
    out_shapes = [shape((LBLK, 4 * HDIM + 128), bf16)] * 4

    def attend_column(state, step, keys, after=()):
        return run(
            functools.partial(column_attend, step),
            state_shapes + (out_shapes if step == 2 else []),
            (place, *queries, *state, *keys),
            flops=4 << 30,
            moved=8 << 20,
            aliases={5: 0, 6: 1, 7: 2},
            after=after,
        )

    state = run(own_kernel, state_shapes, (place, *queries, kv, *ups), flops=4 << 30, moved=8 << 20, after=[totals[0]])
    (plane_total,) = run(
        plane_kernel,
        [shape((NSTATE + 16, 128), bf16)],
        (place, *totals),
        [pltpu.VMEM((4, NSTATE + 16, 128), bf16)],
        after=[state[1]],
    )
    total_ups = [up_z(plane_total, s) for s in (1, 2, 3)]
    local, decay = run(
        local_kernel,
        ring_grid,
        (place, ordered, cums, states, skip),
        [pltpu.VMEM((NSTATE, SLICE), f32)],
        flops=2 << 30,
        moved=4 << 20,
        after=[plane_total],
    )
    entering = run(
        entering_kernel,
        [shape((NSTATE, 128), bf16)] * 4,
        (place, *totals, *total_ups),
        [pltpu.VMEM((4, NSTATE + 16, 128), bf16), pltpu.VMEM((4, NSTATE, 128), bf16)],
        after=[local],
    )
    state = attend_column(state, -1, [left], [entering[0]])
    entering = [entering[0]] + [shift_x(entering[s], s) for s in (1, 2, 3)]
    mixed = run(
        mixed_kernel,
        [shape((LBLK, SLICE), bf16)] * 4,
        (place, ordered, local, decay, *entering),
        [pltpu.VMEM((NSTATE, SLICE), bf16), pltpu.VMEM((4, LBLK, SLICE), bf16)],
        after=[state[1]],
    )
    state = attend_column(state, 1, [right], [mixed[0]])
    mixed = [mixed[0]] + [shift_y(mixed[s], s) for s in (1, 2, 3)]
    *_, o0, o1, o2, o3 = attend_column(state, 2, opposite, mixed[1:])
    outs = [o0] + [swap_x(one, s) for s, one in ((1, o1), (2, o2), (3, o3))]
    (mamba_out,) = run(norm_kernel, [shape((LBLK, 4 * SLICE), bf16)], (place, *mixed, gates, gain), after=[o0])
    (attn_out,) = run(merge_kernel, [shape((LBLK, 8 * HDIM), bf16)], (place, *outs))
    return (mamba_out, attn_out)


def solution(mesh):
    in_specs = (
        P("ctx", "tp"),
        P("ctx", "tp"),
        P("ctx", "tp"),
        P("ctx", "tp"),
        P("ctx", "tp"),
        P("tp"),
        P("tp"),
        P("ctx", "tp"),
        P("ctx", "tp"),
        P("ctx", "tp"),
    )
    out_specs = (P("ctx", "tp"), P("ctx", "tp"))
    return jax.shard_map(on_device, mesh=mesh, in_specs=in_specs, out_specs=out_specs, check_vma=False)
```

```python
import functools

import jax
import jax.numpy as jnp
from jax import lax
from jax.experimental import pallas as pl
from jax.experimental.pallas import tpu as pltpu
from jax.sharding import PartitionSpec as P

MHDIM = 64
NSTATE = 256
HDIM = 128
LBLK = 128
SLICE = 512
KVW = 2 * HDIM
AT_B = SLICE
AT_C = AT_B + NSTATE
AT_DECAY = AT_C + NSTATE
WIDTH = AT_DECAY + 128

eps_norm = 1e-05
neg_large = -1e30
no_top = -1e29
score_scale = HDIM ** (-0.5) * 1.4426950408889634

bf16 = jnp.bfloat16
f32 = jnp.float32


def shape(dims, dtype):
    return jax.ShapeDtypeStruct(dims, dtype)


def run(kernel, outs, args, scratch=(), flops=1000000, moved=1000000, aliases=None, after=()):
    vmem = pl.BlockSpec(memory_space=pltpu.VMEM)
    smem = pl.BlockSpec(memory_space=pltpu.SMEM)
    held = len(args)

    def body(*refs):
        kernel(*refs[:held], *refs[held + len(after) :])

    return pl.pallas_call(
        body if after else kernel,
        out_shape=outs,
        in_specs=[smem] + [vmem] * (held - 1) + [pl.BlockSpec(memory_space=pl.ANY)] * len(after),
        out_specs=[vmem] * len(outs),
        scratch_shapes=list(scratch),
        input_output_aliases=aliases or {},
        compiler_params=pltpu.CompilerParams(vmem_limit_bytes=24 * 1024 * 1024),
        cost_estimate=pl.CostEstimate(flops=flops, bytes_accessed=moved, transcendentals=0),
    )(*args, *after)


def ring4(place, shift):
    return lax.bitwise_and(place + shift, 3)


def lanes(start, size):
    return pl.ds(pl.multiple_of(start * size, size), size)


def split3(vals):
    high = vals.astype(bf16)
    rest = vals - high.astype(f32)
    mid = rest.astype(bf16)
    low = (rest - mid.astype(f32)).astype(bf16)
    return high, mid, low


def iota(dims, dim):
    return lax.broadcasted_iota(jnp.int32, dims, dim)


def pack_kernel(decay, x, b, c, *outs):
    y = lax.bitwise_and(lax.axis_index("ctx").astype(jnp.int32), 3)
    lane = iota((LBLK, 128), 1)
    for s, out in enumerate(outs):
        j = ring4(y, s)
        group = lax.shift_right_logical(j, 1)
        out[:, 0:SLICE] = x[:, lanes(j, SLICE)]
        out[:, AT_B:AT_C] = b[:, lanes(group, NSTATE)]
        out[:, AT_C:AT_DECAY] = c[:, lanes(group, NSTATE)]
        high, mid, low = (part.astype(f32) for part in split3(decay[:, lanes(j, 128)]))
        out[:, AT_DECAY:] = jnp.where(lane < 8, high, jnp.where(lane < 16, mid, low)).astype(bf16)


def pair_kernel(place, own, swapped, out):
    out[0:LBLK, :] = own[...]
    out[LBLK:, :] = swapped[:, :KVW]


def write_total(out, state, log_total):
    out[0:NSTATE, :] = state.astype(bf16)
    high, mid, low = split3(log_total)
    row = iota((16, log_total.shape[1]), 0)
    out[NSTATE:, :] = jnp.where(
        row == 0,
        high.astype(f32),
        jnp.where(row == 1, mid.astype(f32), jnp.where(row == 2, low.astype(f32), 0.0)),
    ).astype(bf16)


def read_total(vals):
    tail = vals[NSTATE:, :].astype(f32)
    return vals[0:NSTATE, :].astype(f32), tail[0:1] + tail[1:2] + tail[2:3]


def total_kernel(place, r0, r1, r2, r3, t0, t1, t2, t3, ordered, cums, states, total):
    x, y = place[1], place[2]
    for s, r in enumerate((r0, r1, r2, r3)):
        ordered[ring4(y, -s)] = r[...]
    tri = (iota((LBLK, LBLK), 0) >= iota((LBLK, LBLK), 1)).astype(f32).astype(bf16)
    cum_parts = jnp.concatenate(
        [jnp.dot(tri, ordered[block, :, AT_DECAY:], preferred_element_type=f32) for block in range(4)], axis=0
    )
    row = iota((128, SLICE), 0)
    head = lax.shift_right_logical(iota((128, SLICE), 1), 6)
    spread = jnp.where((lax.bitwise_and(row, 7) == head) & (row < 24), 1.0, 0.0).astype(bf16)
    cum_all = functools.reduce(
        jnp.add, [jnp.dot(part, spread, preferred_element_type=f32) for part in split3(cum_parts)]
    )
    log_total = jnp.zeros((1, SLICE), f32)
    for block in range(4):
        cum = cum_all[block * LBLK : (block + 1) * LBLK]
        last = cum[LBLK - 1 : LBLK, :]
        cums[block] = cum
        decayed = (ordered[block, :, 0:SLICE].astype(f32) * jnp.exp(last - cum)).astype(bf16)
        state = lax.dot_general(
            ordered[block, :, AT_B:AT_C], decayed, (((0,), (0,)), ((), ())), preferred_element_type=f32
        )
        states[block] = state
        log_total = log_total + last
        total[...] = state if block == 0 else jnp.exp(last) * total[...] + state
    for s, t in enumerate((t0, t1, t2, t3)):
        j = ring4(x, s)
        log_part = jnp.where(
            j == 0,
            log_total[:, 0:128],
            jnp.where(j == 1, log_total[:, 128:256], jnp.where(j == 2, log_total[:, 256:384], log_total[:, 384:512])),
        )
        write_total(t, total[:, lanes(j, 128)], log_part)


def local_kernel(place, ordered, cums, states, skip, local, decay, held):
    gain = skip[:, lanes(place[2], SLICE)]
    causal = iota((LBLK, LBLK), 0) >= iota((LBLK, LBLK), 1)
    tri = causal.astype(f32).astype(bf16)
    low_half = iota((LBLK, 128), 1) < MHDIM
    before = jnp.zeros((1, SLICE), f32)
    for block in range(4):
        cum = cums[block]
        last = cum[LBLK - 1 : LBLK, :]
        decay[block] = jnp.exp(cum + before)
        before = before + last
        parts = ordered[block, :, AT_DECAY:]
        row_parts = lax.dot_general(parts, tri, (((0,), (1,)), ((), ())), preferred_element_type=f32)
        cum_rows = row_parts[0:8] + row_parts[8:16] + row_parts[16:24]
        read = ordered[block, :, AT_C:AT_DECAY]
        pair_dots = lax.dot_general(
            read, ordered[block, :, AT_B:AT_C], (((1,), (1,)), ((), ())), preferred_element_type=f32
        )
        if block == 0:
            held[...] = states[0]
        else:
            state = held[...]
            high = state.astype(bf16)
            low = (state - high.astype(f32)).astype(bf16)
            inflow = jnp.dot(read, high, preferred_element_type=f32) + jnp.dot(read, low, preferred_element_type=f32)
            if block < 3:
                held[...] = jnp.exp(last) * state + states[block]
        for pair in range(4):
            part = slice(pair * 128, pair * 128 + 128)
            xs = ordered[block, :, part]
            sums = []
            for head in (2 * pair, 2 * pair + 1):
                gap = cum[:, head * MHDIM : head * MHDIM + 1] - cum_rows[head : head + 1, :]
                weight = (jnp.exp(jnp.where(causal, gap, neg_large)) * pair_dots).astype(bf16)
                sums.append(jnp.dot(weight, xs, preferred_element_type=f32))
            vals = jnp.where(low_half, sums[0], sums[1]) + gain[:, part] * xs.astype(f32)
            if block > 0:
                vals = vals + jnp.exp(cum[:, part]) * inflow[:, part]
            local[block, :, part] = vals


def plane_kernel(place, r0, r1, r2, r3, column, out, later_column, ordered):
    x = place[1]
    later_column[...] = column[...]
    for s, r in enumerate((r0, r1, r2, r3)):
        ordered[ring4(x, -s)] = r[...]
    total, log_total = read_total(ordered[0])
    for block in range(1, 4):
        state, last = read_total(ordered[block])
        total = jnp.exp(last) * total + state
        log_total = log_total + last
    write_total(out, total, log_total)


def entering_kernel(place, r0, r1, r2, r3, up1, up2, up3, g0, g1, g2, g3, ordered, entering):
    x = place[1]
    for s, r in enumerate((r0, r1, r2, r3)):
        ordered[ring4(x, -s)] = r[...]
    current = jnp.zeros((NSTATE, 128), f32)
    for distance, up in ((3, up3), (2, up2), (1, up1)):
        state, last = read_total(up[...])
        current = jnp.where(place[0] >= distance, jnp.exp(last) * current + state, 0.0)
    for block in range(4):
        entering[block] = current.astype(bf16)
        if block < 3:
            state, last = read_total(ordered[block])
            current = jnp.exp(last) * current + state
    for s, g in enumerate((g0, g1, g2, g3)):
        g[...] = entering[ring4(x, s)]


def mixed_kernel(place, ordered, local, decay, g0, g1, g2, g3, m0, m1, m2, m3, carried, results):
    x, y = place[1], place[2]
    for s, g in enumerate((g0, g1, g2, g3)):
        carried[:, lanes(ring4(x, -s), 128)] = g[...]
    for block in range(4):
        inflow = jnp.dot(ordered[block, :, AT_C:AT_DECAY], carried[...], preferred_element_type=f32)
        results[block] = (local[block] + decay[block] * inflow).astype(bf16)
    for s, m in enumerate((m0, m1, m2, m3)):
        m[...] = results[ring4(y, s)]


def silu_kernel(place, gate, out):
    gates = gate[...].astype(f32)
    out[...] = gates / (1.0 + jnp.exp(-gates))


def norm_kernel(place, m0, m1, m2, m3, gates, gain, out):
    y = place[2]
    gated, squares, groups, slots = [], [], [], []
    for s, m in enumerate((m0, m1, m2, m3)):
        j = ring4(y, -s)
        vals = m[...].astype(f32) * gates[:, lanes(j, SLICE)]
        gated.append(vals)
        squares.append(jnp.sum(vals * vals, axis=1, keepdims=True))
        groups.append(lax.shift_right_logical(j, 1))
        slots.append(j)
    for s in range(4):
        total = jnp.zeros((LBLK, 1), f32)
        for other in range(4):
            total = total + jnp.where(groups[other] == groups[s], squares[other], 0.0)
        factor = lax.rsqrt(total * (1.0 / 1024.0) + eps_norm)
        out[:, lanes(slots[s], SLICE)] = (gated[s] * factor * gain[:, lanes(slots[s], SLICE)]).astype(bf16)


def query_tile(queries, tile):
    one, head = queries[tile // 4], tile % 4
    start = one.shape[1] - (4 - head) * HDIM
    return one[:, start : start + HDIM]


def with_ones(value):
    return jnp.concatenate([value, jnp.ones_like(value)], axis=1)


def attend(tile, queries, keys, values, state, limit=None):
    tops, sums, acc = state
    rows = slice(tile * LBLK, (tile + 1) * LBLK)
    scores = [
        lax.dot_general(queries, key, (((1,), (1,)), ((), ())), preferred_element_type=f32) for key in keys
    ]
    if limit is not None:
        scores = limit(scores)
    top = functools.reduce(jnp.maximum, scores)
    held_top = tops[rows, 0:1]
    new_top = jnp.maximum(held_top, jnp.max(top, axis=1, keepdims=True))
    expos = [jnp.exp2((score - new_top) * score_scale).astype(bf16) for score in scores]
    factor = jnp.exp2((held_top - new_top) * score_scale)
    summed = functools.reduce(
        jnp.add, [jnp.dot(expo, value, preferred_element_type=f32) for expo, value in zip(expos, values)]
    )
    tops[rows, :] = jnp.broadcast_to(new_top, (LBLK, 128))
    sums[rows, :] = sums[rows, :] * factor + summed[:, HDIM:]
    acc[rows, :] = acc[rows, :] * factor + summed[:, :HDIM]


def offset(visible):
    return jnp.where(visible, 0.0, neg_large).astype(f32)


def add_offsets(scores, offsets):
    return [score + one for score, one in zip(scores, offsets)]


def every_tile(place, queries, keys, values, state, own_plane):
    offsets = [offset(place[0] >= distance) for distance in (1, 2, 3)]
    for tile in range(16):

        def limit(scores, slot=tile // 4):
            return [own_plane(scores[0], slot)] + add_offsets(scores[1:], offsets)

        attend(tile, query_tile(queries, tile), keys, values, state, limit)


def own_kernel(place, q0, q1, q2, q3, kv0, kv1, kv2, kv3, tops, sums, acc):
    x = place[1]
    tops[...] = jnp.full(tops.shape, no_top, f32)
    sums[...] = jnp.zeros(sums.shape, f32)
    acc[...] = jnp.zeros(acc.shape, f32)
    blocks = (kv0, kv1, kv2, kv3)
    keys = [kv[:, :HDIM] for kv in blocks]
    values = [with_ones(kv[:, HDIM:]) for kv in blocks]
    lane = iota((LBLK, KVW), 1)
    key_pos = jnp.where(lane < LBLK, x, lax.bitwise_xor(x, 1)) * LBLK + lax.bitwise_and(lane, LBLK - 1)
    ahead = key_pos - iota((LBLK, KVW), 0)

    def own_plane(score, slot):
        return jnp.where(ahead <= lax.bitwise_xor(x, slot) * LBLK, score, neg_large)

    every_tile(place, (q0, q1, q2, q3), keys, values, (tops, sums, acc), own_plane)


def column_attend(step, place, q0, q1, q2, q3, old_tops, old_sums, old_acc, *refs):
    column, outs = refs[0], refs[1:]
    state = outs[:3]
    x, y = place[1], place[2]
    other = ring4(y, step)
    blocks = [column[plane * KVW : (plane + 1) * KVW, :] for plane in range(4)]
    keys = [kv[:, :HDIM] for kv in blocks]
    values = [with_ones(kv[:, HDIM:]) for kv in blocks]
    lane = iota((1, KVW), 1)

    def own_plane(score, slot):
        query_block = lax.bitwise_xor(x, slot) * 4 + y
        near, far = (offset(one * 4 + other < query_block) for one in (x, lax.bitwise_xor(x, 1)))
        return score + jnp.where(lane < LBLK, near, far)

    every_tile(place, (q0, q1, q2, q3), keys, values, state, own_plane)
    if step == 2:
        tops, sums, acc = state
        lane = iota((LBLK, 128), 1)
        for s, o in enumerate(outs[3:]):
            stats = jnp.zeros((LBLK, 128), f32)
            for head in range(4):
                start = (s * 4 + head) * LBLK
                rows = slice(start, start + LBLK)
                total = sums[rows, :]
                o[:, head * HDIM : (head + 1) * HDIM] = (acc[rows, :] / jnp.where(total > 0, total, 1.0)).astype(bf16)
                stats = jnp.where(lane == head * 6, tops[rows, :], jnp.where(lane == head * 6 + 3, total, stats))
            high, mid, low = (part.astype(f32) for part in split3(stats))
            o[:, 4 * HDIM :] = (high + pltpu.roll(mid, 1, 1) + pltpu.roll(low, 2, 1)).astype(bf16)


def merge_kernel(place, o0, o1, o2, o3, out):
    head_group = lax.bitwise_and(place[1], 1)
    for pair, group in (((o0, o2), head_group), ((o1, o3), 1 - head_group)):
        tops, sums = [], []
        for part in pair:
            stats = part[:, 4 * HDIM :].astype(f32)
            stats = stats + pltpu.roll(stats, 127, 1) + pltpu.roll(stats, 126, 1)
            tops.append(stats)
            sums.append(pltpu.roll(stats, 125, 1))
        top = jnp.maximum(tops[0], tops[1])
        weights = [total * jnp.exp2(jnp.minimum((one - top) * score_scale, 0.0)) for one, total in zip(tops, sums)]
        whole = weights[0] + weights[1]
        shares = [weight / jnp.where(whole > 0, whole, 1.0) for weight in weights]
        for head in range(4):
            cols = slice(head * HDIM, (head + 1) * HDIM)
            vals = [
                part[:, cols].astype(f32) * share[:, head * 6 : head * 6 + 1] for part, share in zip(pair, shares)
            ]
            start = pl.multiple_of(group * (4 * HDIM) + head * HDIM, HDIM)
            out[:, pl.ds(start, HDIM)] = (vals[0] + vals[1]).astype(bf16)


def shift_y(vals, shift):
    return lax.ppermute(vals, "ctx", [(i, (i & ~3) | ((i + shift) & 3)) for i in range(64)])


def shift_x(vals, shift):
    return lax.ppermute(vals, "ctx", [(i, (i & ~12) | ((i + 4 * shift) & 12)) for i in range(64)])


def swap_x(vals, step):
    return lax.ppermute(vals, "ctx", [(i, i ^ (4 * step)) for i in range(64)])


def up_z(vals, shift):
    return lax.ppermute(vals, "ctx", [(i, (i + 16 * shift) & 63) for i in range(64)])


def on_device(
    step_inputs, log_decay, write_vecs, read_vecs, gate_vals, skip_gain, norm_gain, query_rows, key_rows, value_rows
):
    index = lax.axis_index("ctx").astype(jnp.int32)
    place = jnp.stack([index // 16, (index // 4) % 4, index % 4, index])
    decay_copies = jnp.tile(log_decay.reshape(LBLK, 4, 1, 8), (1, 1, 3, 1)).reshape(LBLK, 4, 24)
    decay_grid = jnp.pad(decay_copies, ((0, 0), (0, 0), (0, 104))).reshape(LBLK, 512)
    skip = jnp.repeat(skip_gain, MHDIM).reshape(1, 4 * SLICE)
    gain = norm_gain.reshape(1, 4 * SLICE)

    head = (index // 4) % 2

    def one_head(group):
        parts = [lax.dynamic_slice_in_dim(rows, group * HDIM, HDIM, 1) for rows in (key_rows, value_rows)]
        return jnp.concatenate(parts, axis=1)

    def its_queries(group):
        return lax.dynamic_slice_in_dim(query_rows, group * (4 * HDIM), 4 * HDIM, 1)

    kv_own, q_same, q_other = one_head(head), its_queries(head), its_queries(1 - head)
    swapped = swap_x(jnp.concatenate([one_head(1 - head), q_other], axis=1), 1)
    vmem = pl.BlockSpec(memory_space=pltpu.VMEM)
    rings = pl.pallas_call(
        pack_kernel,
        out_shape=[shape((LBLK, WIDTH), bf16)] * 4,
        in_specs=[vmem] * 4,
        out_specs=[vmem] * 4,
        compiler_params=pltpu.CompilerParams(vmem_limit_bytes=60 * 1024 * 1024),
    )(decay_grid, step_inputs, write_vecs, read_vecs)
    rings = [rings[0]] + [shift_y(rings[s], s) for s in (1, 2, 3)]

    queries = [q_same, swapped, swap_x(q_same, 2), swap_x(q_other, 3)]

    (kv,) = run(pair_kernel, [shape((2 * LBLK, KVW), bf16)], (place, kv_own, swapped), after=[rings[0]])
    up1, up2 = up_z(kv, 1), up_z(kv, 2)
    ups = [up1, up2, up_z(up2, 1)]
    column = jnp.concatenate([kv] + ups, axis=0)
    left, right = shift_y(column, 1), shift_y(column, -1)

    gates = run(silu_kernel, [shape((LBLK, 4 * SLICE), f32)], (place, gate_vals), moved=2 << 20)[0]
    ring_grid = [shape((4, LBLK, SLICE), f32)] * 2
    *totals, ordered, cums, states = run(
        total_kernel,
        [shape((NSTATE + 16, 128), bf16)] * 4
        + [shape((4, LBLK, WIDTH), bf16), ring_grid[0], shape((4, NSTATE, SLICE), f32)],
        (place, *rings),
        [pltpu.VMEM((NSTATE, SLICE), f32)],
        flops=600 << 20,
        moved=2 << 20,
        after=[ups[2], gates],
    )
    totals = [totals[0]] + [shift_x(totals[s], s) for s in (1, 2, 3)]

    rows = 16 * LBLK
    state_shapes = [shape((rows, 128), f32)] * 3
    out_shapes = [shape((LBLK, 4 * HDIM + 128), bf16)] * 4

    def attend_column(state, step, keys, after=()):
        return run(
            functools.partial(column_attend, step),
            state_shapes + (out_shapes if step == 2 else []),
            (place, *queries, *state, *keys),
            flops=4 << 30,
            moved=8 << 20,
            aliases={5: 0, 6: 1, 7: 2},
            after=after,
        )

    state = run(own_kernel, state_shapes, (place, *queries, kv, *ups), flops=4 << 30, moved=8 << 20, after=[totals[0]])
    plane_total, later_column = run(
        plane_kernel,
        [shape((NSTATE + 16, 128), bf16), shape(column.shape, bf16)],
        (place, *totals, column),
        [pltpu.VMEM((4, NSTATE + 16, 128), bf16)],
        after=[state[1]],
    )
    total_ups = [up_z(plane_total, s) for s in (1, 2, 3)]
    local, decay = run(
        local_kernel,
        ring_grid,
        (place, ordered, cums, states, skip),
        [pltpu.VMEM((NSTATE, SLICE), f32)],
        flops=2 << 30,
        moved=4 << 20,
        after=[plane_total],
    )
    entering = run(
        entering_kernel,
        [shape((NSTATE, 128), bf16)] * 4,
        (place, *totals, *total_ups),
        [pltpu.VMEM((4, NSTATE + 16, 128), bf16), pltpu.VMEM((4, NSTATE, 128), bf16)],
        after=[local],
    )
    state = attend_column(state, -1, [left], [entering[0]])
    entering = [entering[0]] + [shift_x(entering[s], s) for s in (1, 2, 3)]
    mixed = run(
        mixed_kernel,
        [shape((LBLK, SLICE), bf16)] * 4,
        (place, ordered, local, decay, *entering),
        [pltpu.VMEM((NSTATE, SLICE), bf16), pltpu.VMEM((4, LBLK, SLICE), bf16)],
        after=[state[1]],
    )
    state = attend_column(state, 1, [right], [mixed[0]])
    mixed = [mixed[0]] + [shift_y(mixed[s], s) for s in (1, 2, 3)]
    *_, o0, o1, o2, o3 = attend_column(state, 2, [shift_y(later_column, 2)], mixed[1:])
    outs = [o0] + [swap_x(one, s) for s, one in ((1, o1), (2, o2), (3, o3))]
    (mamba_out,) = run(norm_kernel, [shape((LBLK, 4 * SLICE), bf16)], (place, *mixed, gates, gain), after=[o0])
    (attn_out,) = run(merge_kernel, [shape((LBLK, 8 * HDIM), bf16)], (place, *outs))
    return (mamba_out, attn_out)


def solution(mesh):
    in_specs = (
        P("ctx", "tp"),
        P("ctx", "tp"),
        P("ctx", "tp"),
        P("ctx", "tp"),
        P("ctx", "tp"),
        P("tp"),
        P("tp"),
        P("ctx", "tp"),
        P("ctx", "tp"),
        P("ctx", "tp"),
    )
    out_specs = (P("ctx", "tp"), P("ctx", "tp"))
    return jax.shard_map(on_device, mesh=mesh, in_specs=in_specs, out_specs=out_specs, check_vma=False)
```

```python
import functools

import jax
import jax.numpy as jnp
from jax import lax
from jax.experimental import pallas as pl
from jax.experimental.pallas import tpu as pltpu
from jax.sharding import PartitionSpec as P

MHDIM = 64
NSTATE = 256
HDIM = 128
LBLK = 128
SLICE = 512
KVW = 2 * HDIM
AT_B = SLICE
AT_C = AT_B + NSTATE
AT_DECAY = AT_C + NSTATE
WIDTH = AT_DECAY + 128

eps_norm = 1e-05
neg_large = -1e30
no_top = -1e29
score_scale = HDIM ** (-0.5) * 1.4426950408889634

bf16 = jnp.bfloat16
f32 = jnp.float32


def shape(dims, dtype):
    return jax.ShapeDtypeStruct(dims, dtype)


def run(kernel, outs, args, scratch=(), flops=1000000, moved=1000000, aliases=None, after=()):
    vmem = pl.BlockSpec(memory_space=pltpu.VMEM)
    smem = pl.BlockSpec(memory_space=pltpu.SMEM)
    held = len(args)

    def body(*refs):
        kernel(*refs[:held], *refs[held + len(after) :])

    return pl.pallas_call(
        body if after else kernel,
        out_shape=outs,
        in_specs=[smem] + [vmem] * (held - 1) + [pl.BlockSpec(memory_space=pl.ANY)] * len(after),
        out_specs=[vmem] * len(outs),
        scratch_shapes=list(scratch),
        input_output_aliases=aliases or {},
        compiler_params=pltpu.CompilerParams(vmem_limit_bytes=24 * 1024 * 1024),
        cost_estimate=pl.CostEstimate(flops=flops, bytes_accessed=moved, transcendentals=0),
    )(*args, *after)


def ring4(place, shift):
    return lax.bitwise_and(place + shift, 3)


def lanes(start, size):
    return pl.ds(pl.multiple_of(start * size, size), size)


def split3(vals):
    high = vals.astype(bf16)
    rest = vals - high.astype(f32)
    mid = rest.astype(bf16)
    low = (rest - mid.astype(f32)).astype(bf16)
    return high, mid, low


def iota(dims, dim):
    return lax.broadcasted_iota(jnp.int32, dims, dim)


def pack_kernel(decay, x, b, c, *outs):
    y = lax.bitwise_and(lax.axis_index("ctx").astype(jnp.int32), 3)
    head, lane = iota((32, 128), 0), iota((32, 128), 1)
    parts = split3(decay[...])
    for s, out in enumerate(outs):
        j = ring4(y, s)
        group = lax.shift_right_logical(j, 1)
        out[:, 0:SLICE] = x[:, lanes(j, SLICE)]
        out[:, AT_B:AT_C] = b[:, lanes(group, NSTATE)]
        out[:, AT_C:AT_DECAY] = c[:, lanes(group, NSTATE)]
        spread = jnp.zeros((LBLK, 128), f32)
        for i, part in enumerate(parts):
            chosen = (head == 8 * j + lax.bitwise_and(lane, 7)) & (lax.shift_right_logical(lane, 3) == i)
            spread = spread + lax.dot_general(
                part,
                jnp.where(chosen, 1.0, 0.0).astype(bf16),
                (((0,), (0,)), ((), ())),
                preferred_element_type=f32,
            )
        out[:, AT_DECAY:] = spread.astype(bf16)


def pair_kernel(place, own, swapped, out):
    out[0:LBLK, :] = own[...]
    out[LBLK:, :] = swapped[:, :KVW]


def write_total(out, state, log_total):
    out[0:NSTATE, :] = state.astype(bf16)
    high, mid, low = split3(log_total)
    row = iota((16, log_total.shape[1]), 0)
    out[NSTATE:, :] = jnp.where(
        row == 0,
        high.astype(f32),
        jnp.where(row == 1, mid.astype(f32), jnp.where(row == 2, low.astype(f32), 0.0)),
    ).astype(bf16)


def read_total(vals):
    tail = vals[NSTATE:, :].astype(f32)
    return vals[0:NSTATE, :].astype(f32), tail[0:1] + tail[1:2] + tail[2:3]


def total_kernel(place, r0, r1, r2, r3, t0, t1, t2, t3, ordered, cums, states, total):
    x, y = place[1], place[2]
    for s, r in enumerate((r0, r1, r2, r3)):
        ordered[ring4(y, -s)] = r[...]
    tri = (iota((LBLK, LBLK), 0) >= iota((LBLK, LBLK), 1)).astype(f32).astype(bf16)
    cum_parts = jnp.concatenate(
        [jnp.dot(tri, ordered[block, :, AT_DECAY:], preferred_element_type=f32) for block in range(4)], axis=0
    )
    row = iota((128, SLICE), 0)
    head = lax.shift_right_logical(iota((128, SLICE), 1), 6)
    spread = jnp.where((lax.bitwise_and(row, 7) == head) & (row < 24), 1.0, 0.0).astype(bf16)
    cum_all = functools.reduce(
        jnp.add, [jnp.dot(part, spread, preferred_element_type=f32) for part in split3(cum_parts)]
    )
    log_total = jnp.zeros((1, SLICE), f32)
    for block in range(4):
        cum = cum_all[block * LBLK : (block + 1) * LBLK]
        last = cum[LBLK - 1 : LBLK, :]
        cums[block] = cum
        decayed = (ordered[block, :, 0:SLICE].astype(f32) * jnp.exp(last - cum)).astype(bf16)
        state = lax.dot_general(
            ordered[block, :, AT_B:AT_C], decayed, (((0,), (0,)), ((), ())), preferred_element_type=f32
        )
        states[block] = state
        log_total = log_total + last
        total[...] = state if block == 0 else jnp.exp(last) * total[...] + state
    for s, t in enumerate((t0, t1, t2, t3)):
        j = ring4(x, s)
        log_part = jnp.where(
            j == 0,
            log_total[:, 0:128],
            jnp.where(j == 1, log_total[:, 128:256], jnp.where(j == 2, log_total[:, 256:384], log_total[:, 384:512])),
        )
        write_total(t, total[:, lanes(j, 128)], log_part)


def local_kernel(place, ordered, cums, states, skip, local, decay, held):
    gain = skip[:, lanes(place[2], SLICE)]
    causal = iota((LBLK, LBLK), 0) >= iota((LBLK, LBLK), 1)
    tri = causal.astype(f32).astype(bf16)
    low_half = iota((LBLK, 128), 1) < MHDIM
    before = jnp.zeros((1, SLICE), f32)
    for block in range(4):
        cum = cums[block]
        last = cum[LBLK - 1 : LBLK, :]
        decay[block] = jnp.exp(cum + before)
        before = before + last
        parts = ordered[block, :, AT_DECAY:]
        row_parts = lax.dot_general(parts, tri, (((0,), (1,)), ((), ())), preferred_element_type=f32)
        cum_rows = row_parts[0:8] + row_parts[8:16] + row_parts[16:24]
        read = ordered[block, :, AT_C:AT_DECAY]
        pair_dots = lax.dot_general(
            read, ordered[block, :, AT_B:AT_C], (((1,), (1,)), ((), ())), preferred_element_type=f32
        )
        if block == 0:
            held[...] = states[0]
        else:
            state = held[...]
            high = state.astype(bf16)
            low = (state - high.astype(f32)).astype(bf16)
            inflow = jnp.dot(read, high, preferred_element_type=f32) + jnp.dot(read, low, preferred_element_type=f32)
            if block < 3:
                held[...] = jnp.exp(last) * state + states[block]
        for pair in range(4):
            part = slice(pair * 128, pair * 128 + 128)
            xs = ordered[block, :, part]
            sums = []
            for head in (2 * pair, 2 * pair + 1):
                gap = cum[:, head * MHDIM : head * MHDIM + 1] - cum_rows[head : head + 1, :]
                weight = (jnp.exp(jnp.where(causal, gap, neg_large)) * pair_dots).astype(bf16)
                sums.append(jnp.dot(weight, xs, preferred_element_type=f32))
            vals = jnp.where(low_half, sums[0], sums[1]) + gain[:, part] * xs.astype(f32)
            if block > 0:
                vals = vals + jnp.exp(cum[:, part]) * inflow[:, part]
            local[block, :, part] = vals


def plane_kernel(place, r0, r1, r2, r3, column, out, later_column, ordered):
    x = place[1]
    later_column[...] = column[...]
    for s, r in enumerate((r0, r1, r2, r3)):
        ordered[ring4(x, -s)] = r[...]
    total, log_total = read_total(ordered[0])
    for block in range(1, 4):
        state, last = read_total(ordered[block])
        total = jnp.exp(last) * total + state
        log_total = log_total + last
    write_total(out, total, log_total)


def entering_kernel(place, r0, r1, r2, r3, up1, up2, up3, g0, g1, g2, g3, ordered, entering):
    x = place[1]
    for s, r in enumerate((r0, r1, r2, r3)):
        ordered[ring4(x, -s)] = r[...]
    current = jnp.zeros((NSTATE, 128), f32)
    for distance, up in ((3, up3), (2, up2), (1, up1)):
        state, last = read_total(up[...])
        current = jnp.where(place[0] >= distance, jnp.exp(last) * current + state, 0.0)
    for block in range(4):
        entering[block] = current.astype(bf16)
        if block < 3:
            state, last = read_total(ordered[block])
            current = jnp.exp(last) * current + state
    for s, g in enumerate((g0, g1, g2, g3)):
        g[...] = entering[ring4(x, s)]


def mixed_kernel(place, ordered, local, decay, g0, g1, g2, g3, m0, m1, m2, m3, carried, results):
    x, y = place[1], place[2]
    for s, g in enumerate((g0, g1, g2, g3)):
        carried[:, lanes(ring4(x, -s), 128)] = g[...]
    for block in range(4):
        inflow = jnp.dot(ordered[block, :, AT_C:AT_DECAY], carried[...], preferred_element_type=f32)
        results[block] = (local[block] + decay[block] * inflow).astype(bf16)
    for s, m in enumerate((m0, m1, m2, m3)):
        m[...] = results[ring4(y, s)]


def silu_kernel(place, gate, out):
    gates = gate[...].astype(f32)
    out[...] = gates / (1.0 + jnp.exp(-gates))


def norm_kernel(place, m0, m1, m2, m3, gates, gain, out):
    y = place[2]
    gated, squares, groups, slots = [], [], [], []
    for s, m in enumerate((m0, m1, m2, m3)):
        j = ring4(y, -s)
        vals = m[...].astype(f32) * gates[:, lanes(j, SLICE)]
        gated.append(vals)
        squares.append(jnp.sum(vals * vals, axis=1, keepdims=True))
        groups.append(lax.shift_right_logical(j, 1))
        slots.append(j)
    for s in range(4):
        total = jnp.zeros((LBLK, 1), f32)
        for other in range(4):
            total = total + jnp.where(groups[other] == groups[s], squares[other], 0.0)
        factor = lax.rsqrt(total * (1.0 / 1024.0) + eps_norm)
        out[:, lanes(slots[s], SLICE)] = (gated[s] * factor * gain[:, lanes(slots[s], SLICE)]).astype(bf16)


def query_tile(queries, tile):
    one, head = queries[tile // 4], tile % 4
    start = one.shape[1] - (4 - head) * HDIM
    return one[:, start : start + HDIM]


def with_ones(value):
    return jnp.concatenate([value, jnp.ones_like(value)], axis=1)


def attend(tile, queries, keys, values, state, limit=None):
    tops, sums, acc = state
    rows = slice(tile * LBLK, (tile + 1) * LBLK)
    scores = [
        lax.dot_general(queries, key, (((1,), (1,)), ((), ())), preferred_element_type=f32) for key in keys
    ]
    if limit is not None:
        scores = limit(scores)
    top = functools.reduce(jnp.maximum, scores)
    held_top = tops[rows, 0:1]
    new_top = jnp.maximum(held_top, jnp.max(top, axis=1, keepdims=True))
    expos = [jnp.exp2((score - new_top) * score_scale).astype(bf16) for score in scores]
    factor = jnp.exp2((held_top - new_top) * score_scale)
    summed = functools.reduce(
        jnp.add, [jnp.dot(expo, value, preferred_element_type=f32) for expo, value in zip(expos, values)]
    )
    tops[rows, :] = jnp.broadcast_to(new_top, (LBLK, 128))
    sums[rows, :] = sums[rows, :] * factor + summed[:, HDIM:]
    acc[rows, :] = acc[rows, :] * factor + summed[:, :HDIM]


def offset(visible):
    return jnp.where(visible, 0.0, neg_large).astype(f32)


def add_offsets(scores, offsets):
    return [score + one for score, one in zip(scores, offsets)]


def every_tile(place, queries, keys, values, state, own_plane, slots=(0, 1, 2, 3)):
    offsets = [offset(place[0] >= distance) for distance in (1, 2, 3)]
    for tile in (slot * 4 + head for slot in slots for head in range(4)):

        def limit(scores, slot=tile // 4):
            return [own_plane(scores[0], slot)] + add_offsets(scores[1:], offsets)

        attend(tile, query_tile(queries, tile), keys, values, state, limit)


def own_kernel(place, q0, q1, q2, q3, kv0, kv1, kv2, kv3, tops, sums, acc):
    x = place[1]
    tops[...] = jnp.full(tops.shape, no_top, f32)
    sums[...] = jnp.zeros(sums.shape, f32)
    acc[...] = jnp.zeros(acc.shape, f32)
    blocks = (kv0, kv1, kv2, kv3)
    keys = [kv[:, :HDIM] for kv in blocks]
    values = [with_ones(kv[:, HDIM:]) for kv in blocks]
    lane = iota((LBLK, KVW), 1)
    key_pos = jnp.where(lane < LBLK, x, lax.bitwise_xor(x, 1)) * LBLK + lax.bitwise_and(lane, LBLK - 1)
    ahead = key_pos - iota((LBLK, KVW), 0)

    def own_plane(score, slot):
        return jnp.where(ahead <= lax.bitwise_xor(x, slot) * LBLK, score, neg_large)

    every_tile(place, (q0, q1, q2, q3), keys, values, (tops, sums, acc), own_plane)


def column_attend(step, slots, place, q0, q1, q2, q3, old_tops, old_sums, old_acc, *refs):
    column, outs = refs[0], refs[1:]
    state = outs[:3]
    x, y = place[1], place[2]
    other = ring4(y, step)
    blocks = [column[plane * KVW : (plane + 1) * KVW, :] for plane in range(4)]
    keys = [kv[:, :HDIM] for kv in blocks]
    values = [with_ones(kv[:, HDIM:]) for kv in blocks]
    lane = iota((1, KVW), 1)

    def own_plane(score, slot):
        query_block = lax.bitwise_xor(x, slot) * 4 + y
        near, far = (offset(one * 4 + other < query_block) for one in (x, lax.bitwise_xor(x, 1)))
        return score + jnp.where(lane < LBLK, near, far)

    every_tile(place, (q0, q1, q2, q3), keys, values, state, own_plane, slots)
    if step == 2:
        tops, sums, acc = state
        lane = iota((LBLK, 128), 1)
        for s, o in zip(slots, outs[3:]):
            stats = jnp.zeros((LBLK, 128), f32)
            for head in range(4):
                start = (s * 4 + head) * LBLK
                rows = slice(start, start + LBLK)
                total = sums[rows, :]
                o[:, head * HDIM : (head + 1) * HDIM] = (acc[rows, :] / jnp.where(total > 0, total, 1.0)).astype(bf16)
                stats = jnp.where(lane == head * 6, tops[rows, :], jnp.where(lane == head * 6 + 3, total, stats))
            high, mid, low = (part.astype(f32) for part in split3(stats))
            o[:, 4 * HDIM :] = (high + pltpu.roll(mid, 1, 1) + pltpu.roll(low, 2, 1)).astype(bf16)


def merge_kernel(place, o0, o1, o2, o3, out):
    head_group = lax.bitwise_and(place[1], 1)
    for pair, group in (((o0, o2), head_group), ((o1, o3), 1 - head_group)):
        tops, sums = [], []
        for part in pair:
            stats = part[:, 4 * HDIM :].astype(f32)
            stats = stats + pltpu.roll(stats, 127, 1) + pltpu.roll(stats, 126, 1)
            tops.append(stats)
            sums.append(pltpu.roll(stats, 125, 1))
        top = jnp.maximum(tops[0], tops[1])
        weights = [total * jnp.exp2(jnp.minimum((one - top) * score_scale, 0.0)) for one, total in zip(tops, sums)]
        whole = weights[0] + weights[1]
        shares = [weight / jnp.where(whole > 0, whole, 1.0) for weight in weights]
        for head in range(4):
            cols = slice(head * HDIM, (head + 1) * HDIM)
            vals = [
                part[:, cols].astype(f32) * share[:, head * 6 : head * 6 + 1] for part, share in zip(pair, shares)
            ]
            start = pl.multiple_of(group * (4 * HDIM) + head * HDIM, HDIM)
            out[:, pl.ds(start, HDIM)] = (vals[0] + vals[1]).astype(bf16)


def shift_y(vals, shift):
    return lax.ppermute(vals, "ctx", [(i, (i & ~3) | ((i + shift) & 3)) for i in range(64)])


def shift_x(vals, shift):
    return lax.ppermute(vals, "ctx", [(i, (i & ~12) | ((i + 4 * shift) & 12)) for i in range(64)])


def swap_x(vals, step):
    return lax.ppermute(vals, "ctx", [(i, i ^ (4 * step)) for i in range(64)])


def up_z(vals, shift):
    return lax.ppermute(vals, "ctx", [(i, (i + 16 * shift) & 63) for i in range(64)])


def on_device(
    step_inputs, log_decay, write_vecs, read_vecs, gate_vals, skip_gain, norm_gain, query_rows, key_rows, value_rows
):
    index = lax.axis_index("ctx").astype(jnp.int32)
    place = jnp.stack([index // 16, (index // 4) % 4, index % 4, index])
    skip = jnp.repeat(skip_gain, MHDIM).reshape(1, 4 * SLICE)
    gain = norm_gain.reshape(1, 4 * SLICE)

    head = (index // 4) % 2

    def one_head(group):
        parts = [lax.dynamic_slice_in_dim(rows, group * HDIM, HDIM, 1) for rows in (key_rows, value_rows)]
        return jnp.concatenate(parts, axis=1)

    def its_queries(group):
        return lax.dynamic_slice_in_dim(query_rows, group * (4 * HDIM), 4 * HDIM, 1)

    kv_own, q_same, q_other = one_head(head), its_queries(head), its_queries(1 - head)
    swapped = swap_x(jnp.concatenate([one_head(1 - head), q_other], axis=1), 1)
    vmem = pl.BlockSpec(memory_space=pltpu.VMEM)
    rings = pl.pallas_call(
        pack_kernel,
        out_shape=[shape((LBLK, WIDTH), bf16)] * 4,
        in_specs=[vmem] * 4,
        out_specs=[vmem] * 4,
        compiler_params=pltpu.CompilerParams(vmem_limit_bytes=60 * 1024 * 1024),
    )(log_decay.T, step_inputs, write_vecs, read_vecs)
    rings = [rings[0]] + [shift_y(rings[s], s) for s in (1, 2, 3)]

    queries = [q_same, swapped, swap_x(q_same, 2), swap_x(q_other, 3)]

    (kv,) = run(pair_kernel, [shape((2 * LBLK, KVW), bf16)], (place, kv_own, swapped), after=[rings[0]])
    up1, up2 = up_z(kv, 1), up_z(kv, 2)
    ups = [up1, up2, up_z(up2, 1)]
    column = jnp.concatenate([kv] + ups, axis=0)
    left, right = shift_y(column, 1), shift_y(column, -1)

    gates = run(silu_kernel, [shape((LBLK, 4 * SLICE), f32)], (place, gate_vals), moved=2 << 20)[0]
    ring_grid = [shape((4, LBLK, SLICE), f32)] * 2
    *totals, ordered, cums, states = run(
        total_kernel,
        [shape((NSTATE + 16, 128), bf16)] * 4
        + [shape((4, LBLK, WIDTH), bf16), ring_grid[0], shape((4, NSTATE, SLICE), f32)],
        (place, *rings),
        [pltpu.VMEM((NSTATE, SLICE), f32)],
        flops=600 << 20,
        moved=2 << 20,
        after=[ups[2], gates],
    )
    totals = [totals[0]] + [shift_x(totals[s], s) for s in (1, 2, 3)]

    rows = 16 * LBLK
    state_shapes = [shape((rows, 128), f32)] * 3
    out_shapes = [shape((LBLK, 4 * HDIM + 128), bf16)] * 4

    def attend_column(state, step, keys, after=(), slots=(0, 1, 2, 3)):
        return run(
            functools.partial(column_attend, step, slots),
            state_shapes + (out_shapes[: len(slots)] if step == 2 else []),
            (place, *queries, *state, *keys),
            flops=len(slots) << 30,
            moved=8 << 20,
            aliases={5: 0, 6: 1, 7: 2},
            after=after,
        )

    state = run(own_kernel, state_shapes, (place, *queries, kv, *ups), flops=4 << 30, moved=8 << 20, after=[totals[0]])
    plane_total, later_column = run(
        plane_kernel,
        [shape((NSTATE + 16, 128), bf16), shape(column.shape, bf16)],
        (place, *totals, column),
        [pltpu.VMEM((4, NSTATE + 16, 128), bf16)],
        after=[state[1]],
    )
    total_ups = [up_z(plane_total, s) for s in (1, 2, 3)]
    local, decay = run(
        local_kernel,
        ring_grid,
        (place, ordered, cums, states, skip),
        [pltpu.VMEM((NSTATE, SLICE), f32)],
        flops=2 << 30,
        moved=4 << 20,
        after=[plane_total],
    )
    entering = run(
        entering_kernel,
        [shape((NSTATE, 128), bf16)] * 4,
        (place, *totals, *total_ups),
        [pltpu.VMEM((4, NSTATE + 16, 128), bf16), pltpu.VMEM((4, NSTATE, 128), bf16)],
        after=[local],
    )
    state = attend_column(state, -1, [left], [entering[0]])
    entering = [entering[0]] + [shift_x(entering[s], s) for s in (1, 2, 3)]
    mixed = run(
        mixed_kernel,
        [shape((LBLK, SLICE), bf16)] * 4,
        (place, ordered, local, decay, *entering),
        [pltpu.VMEM((NSTATE, SLICE), bf16), pltpu.VMEM((4, LBLK, SLICE), bf16)],
        after=[state[1]],
    )
    state = attend_column(state, 1, [right], [mixed[0]])
    mixed = [mixed[0]] + [shift_y(mixed[s], s) for s in (1, 2, 3)]
    opposite = shift_y(later_column, 2)
    *state, o1, o2, o3 = attend_column(state, 2, [opposite], mixed[1:], (1, 2, 3))
    *_, o0 = attend_column(state, 2, [opposite], [], (0,))
    outs = [o0] + [swap_x(one, s) for s, one in ((1, o1), (2, o2), (3, o3))]
    (mamba_out,) = run(norm_kernel, [shape((LBLK, 4 * SLICE), bf16)], (place, *mixed, gates, gain), after=[o0])
    (attn_out,) = run(merge_kernel, [shape((LBLK, 8 * HDIM), bf16)], (place, *outs))
    return (mamba_out, attn_out)


def solution(mesh):
    in_specs = (
        P("ctx", "tp"),
        P("ctx", "tp"),
        P("ctx", "tp"),
        P("ctx", "tp"),
        P("ctx", "tp"),
        P("tp"),
        P("tp"),
        P("ctx", "tp"),
        P("ctx", "tp"),
        P("ctx", "tp"),
    )
    out_specs = (P("ctx", "tp"), P("ctx", "tp"))
    return jax.shard_map(on_device, mesh=mesh, in_specs=in_specs, out_specs=out_specs, check_vma=False)
```
